32 devices in a mesh: group: 2 (over y), gx: 4 (over z), gy: 2 (over x), gz: 2 (over core).
Axes of the slice: x: 2, y: 2, z: 4, core: 2. Of those that a mesh axis runs over, the one named last changes fastest.
Arguments:
- base_state: float32 [16, 8, 384, 256], P('group', 'gz', 'gx', 'gy'), parts along dimension 0, may hold values from -6 to 6
- tendency: bfloat16 [16, 8, 384, 256], P('group', 'gz', 'gx', 'gy'), parts along dimension 0, may hold values from -6 to 6
- inflow: float32 [4, 18432], P('group', ('gx', 'gy')), parts along dimension 0, may hold values from 0.5 to 2
- chord_len: float32 [36864], P(('group', 'gx', 'gy')), parts along dimension 0, may hold values from 2 to 6
- twist_base: float32 [36864], P(('group', 'gx', 'gy')), parts along dimension 0, may hold values from 0 to 0.4
- compliance: float32 [36864], P(('group', 'gx', 'gy')), parts along dimension 0, may hold values from 0.005 to 0.05
- blade_frame: float32 [32, 18432], P('group', ('gx', 'gy')), parts along dimension 0, may hold values from -6 to 6
- owner_tile: int32 [18432, 2], P(('gx', 'gy'), 'group'), parts along dimension 1, may hold values from 0 to 7; in each aligned block of 2304 rows (0 to 2303, 2304 to 4607, ...) at most 576 rows name the same one
- point_cells: int32 [6, 18432], P('group', ('gx', 'gy')), parts along dimension 0, may hold values from 0 to 127, as said below
Outputs:
- forced_state: float32 [16, 8, 384, 256], P('group', 'gz', 'gx', 'gy'), parts along dimension 0
- divergence_lines: float32 [16, 256, 384], P(('group', 'gz'), ('gy', 'gx')), parts along dimension 0
The draws below stay inside these ranges and needn't reach their ends.
There are 2 independent parts, one for each index of `group`. The reference program is written for one: setup_inputs(seed, part) draws one part's arguments, and reference() takes and returns one part's arrays. A program takes and returns all parts, laid end to end along the dimension named above; each array names one. Nothing has to cross between parts.
Inputs may be any that keep to these rules, and one draw needn't show every extreme that they name: `owner_tile`: within the points of one device (aligned blocks of 2304 points), no tile is named by more than 576 points, a bound that some block reaches. `point_cells`: row 0 is the x cell within the owning tile (below 96), row 1 the y cell within it (below 128), row 2 the global z level (below 8).
All inputs are finite; a program needn't handle non-finite values.
Results may differ from the reference program's by a relative error of at most 0.00056.
Values sent between devices are 32-bit elements; how exact they have to be, the bound alone decides.
A program may use at most 64 MiB of HBM per device.

```python
import math
import jax
import jax.numpy as jnp
import numpy as np
from jax import lax

C = 8
CX = 96
CY = 128
P_DEV = 2304
TILES = 8
POINTS = 18432
CAP = 576
NX = 384
NY = 256
NZ = 8
N_GX = 4
N_GY = 2


def draw_point_cells(key, part):
    key_x, key_y, key_z = jax.random.split(key, 3)
    x_cells = jax.random.randint(key_x, (POINTS,), 0, CX)
    y_cells = jax.random.randint(key_y, (POINTS,), 0, CY)
    z_cells = jax.random.randint(key_z, (POINTS,), 0, NZ)
    x_cells = x_cells.at[0].set(CX - 1)
    y_cells = y_cells.at[0].set(CY - 1)
    return jnp.stack([x_cells, y_cells, z_cells]).astype(jnp.int32)


def levels(key, extent, cuts, least, top_value):
    level = 1.0
    for dim, shards_of in cuts:
        draws = jax.random.uniform(jax.random.fold_in(jax.random.fold_in(key, 6), dim), (shards_of,), jnp.float32, least / len(cuts), top_value / len(cuts))
        level = level * jnp.repeat(jnp.exp(draws), extent[dim] // shards_of).reshape((-1,) + (1,) * (len(extent) - 1 - dim))
    return level


def assign_block(own_key, own, number, rows, count, top, limit, slope):
    sequence = jax.random.permutation(own_key, count)
    heavy_load, usual = load_shares(count, rows * top, limit, slope, True), load_shares(count, rows * top, limit, slope, False)
    places = jnp.arange(count)

    def named(lengths, offset_by):
        used = int((lengths > 0).sum())
        fixed = max(1, used // 4)
        passed = fixed + (places - fixed + offset_by * (used - fixed)) % max(1, count - fixed)
        return jnp.zeros((count,), jnp.int32).at[sequence[jnp.where(places < fixed, places, passed)]].set(jnp.asarray(lengths, jnp.int32))

    lengths = jnp.where(number % 4 == 0, named(heavy_load, number // 4), named(usual, number - number // 4 - 1))
    mixed = jax.random.permutation(jax.random.fold_in(own, 3), count)
    giver, taker = mixed[0:count // 2 * 2:2], mixed[1:count // 2 * 2:2]
    margin = jnp.minimum(lengths[giver] - 1, limit - lengths[taker]) // 2
    margin = jnp.where((giver == sequence[0]) | (taker == sequence[0]) | (lengths[taker] == 0), 0, jnp.maximum(margin, 0))
    passed = jax.random.randint(jax.random.fold_in(own, 4), (count // 2,), 0, 1 << 20) % (margin + 1)
    lengths = lengths.at[giver].add(-passed).at[taker].add(passed)
    items = jnp.searchsorted(jnp.cumsum(lengths), jnp.arange(rows * top), side="right").astype(jnp.int32)
    table = items.reshape(top, rows).T
    table = table[jax.random.permutation(jax.random.fold_in(own, 1), rows)]
    offset_by = jax.random.randint(jax.random.fold_in(own, 2), (rows, 1), 0, top)
    return jnp.take_along_axis(table, (jnp.arange(top)[None, :] + offset_by) % top, axis=1)


def load_shares(number_of, total, bound, slope, full):
    loads = [(1 << 20) // math.isqrt(standing ** slope) + 1 for standing in range(1, number_of + 1)]
    largest = bound if full else min(bound, max(-(-total // number_of), total * loads[0] // sum(loads)))
    least = 1 if total - largest >= number_of - 1 else 0
    holding, surplus = [largest] + [least] * (number_of - 1), total - largest - least * (number_of - 1)
    while surplus > 0:
        candidates = [i for i in range(1, number_of) if holding[i] < largest] or [i for i in range(1, number_of) if holding[i] < bound]
        pool, budget = sum([loads[i] for i in candidates]), surplus
        for i in candidates:
            more = min(bound - holding[i], max(1, budget * loads[i] // pool), surplus)
            holding[i] = holding[i] + more
            surplus = surplus - more
    return np.array(holding)


def centred(rng, dims, deviation, bound, pieces=(), kind=jnp.bfloat16):
    drawn = jax.random.normal(rng, dims, jnp.float32) * deviation
    if len(pieces) > 0:
        drawn = levels(rng, dims, pieces, -0.22, 0.18) * drawn
    return jnp.clip(drawn, min=-bound, max=bound).astype(kind)


def setup_inputs(seed: int = 0, part: int = 0) -> dict:
    arg_keys = jax.random.split(jax.random.key(seed), 10)
    own_keys = jax.random.split(jax.random.fold_in(arg_keys[9], part), 10)
    base_state = centred(own_keys[0], (C, NZ, NX, NY), 1.0, 6.0, ((1, 2), (2, 4), (3, 2)), jnp.float32)
    tendency = centred(own_keys[1], (C, NZ, NX, NY), 1.0, 6.0, ((1, 2), (2, 4), (3, 2)))
    inflow = jnp.clip(0.5 + 1.5 * jax.random.uniform(own_keys[2], (2, POINTS), jnp.float32) ** levels(own_keys[2], (2, POINTS), ((1, 8),), -0.2, 0.2), 0.5, 2.0)
    chord_len = jnp.clip(2.0 + 4.0 * jax.random.uniform(own_keys[3], (POINTS,), jnp.float32) ** levels(own_keys[3], (POINTS,), ((0, 8),), -0.2, 0.2), 2.0, 6.0)
    twist_base = jnp.clip(0.4 * jax.random.uniform(own_keys[4], (POINTS,), jnp.float32) ** levels(own_keys[4], (POINTS,), ((0, 8),), -0.2, 0.2), 0.0, 0.4)
    compliance = jnp.clip(jnp.exp(math.log(0.05) - 2.3025851 * jax.random.uniform(own_keys[5], (POINTS,), jnp.float32) ** levels(own_keys[5], (POINTS,), ((0, 8),), -0.2, 0.2)), 0.005, 0.05)
    blade_frame = centred(own_keys[6], (2 * C, POINTS), 1.0, 6.0, ((1, 8),), jnp.float32)
    owner_tile_keys = jax.random.split(jax.random.fold_in(own_keys[7], 1), POINTS // P_DEV)
    owner_tile_turns = jax.random.permutation(jax.random.fold_in(own_keys[7], 3), POINTS // P_DEV)
    owner_tile = jax.vmap(lambda own, number: assign_block(jax.random.fold_in(own_keys[7], 2), own, number, P_DEV, TILES, 1, CAP, 2))(owner_tile_keys, owner_tile_turns).reshape((POINTS, 1))
    point_cells = draw_point_cells(jax.random.fold_in(jax.random.fold_in(arg_keys[9], part), 71), part)
    return {"base_state": base_state, "tendency": tendency, "inflow": inflow, "chord_len": chord_len, "twist_base": twist_base, "compliance": compliance, "blade_frame": blade_frame, "owner_tile": owner_tile, "point_cells": point_cells}


sigma_xy = 3.0
sigma_z = 1.5
reach_cells = 8
tap_total = sum([math.exp(-(float(offset_cell) / sigma_xy) ** 2) for offset_cell in range(-8, 9)])


def tap_weight(offset):
    scaled = offset.astype(jnp.float32) / sigma_xy
    return jnp.where(jnp.abs(offset) <= reach_cells, jnp.exp(-scaled * scaled) / tap_total, 0.0)


def point_forces(inflow, chord_len, twist_base, compliance, blade_frame):
    normal = inflow[0]
    tangent = inflow[1]
    speed_sq = normal * normal + tangent * tangent
    twist_angle = twist_base + compliance * speed_sq
    attack = jnp.arctan2(normal, tangent) - twist_angle
    pressure = 0.5 * speed_sq * chord_len
    lift_force = pressure * (2.0 * math.pi) * jnp.sin(attack)
    drag_force = pressure * (0.01 + 0.5 * attack * attack)
    half = blade_frame.shape[0] // 2
    return blade_frame[:half] * lift_force[None, :] + blade_frame[half:] * drag_force[None, :]


def slot_rows(owners, tiles, capacity):
    onehot = (owners[:, None] == jnp.arange(tiles, dtype=jnp.int32)[None, :]).astype(jnp.int32)
    earlier = jnp.cumsum(onehot, axis=0) - onehot
    position = jnp.sum(earlier * onehot, axis=1)
    return owners * capacity + position


def pack_points(forces, point_cells, owners, tiles, capacity):
    slot_index = slot_rows(owners, tiles, capacity)
    slot_count = tiles * capacity
    force_rows = jnp.zeros((forces.shape[0], slot_count), jnp.float32).at[:, slot_index].set(forces)
    cell_rows = jnp.zeros((3, slot_count), jnp.int32).at[:, slot_index].set(point_cells)
    return force_rows, cell_rows


def smear_tile(force_rows, cell_rows, first_level, levels_here, levels_all, width_x, width_y):
    x_local = cell_rows[0]
    y_local = cell_rows[1]
    z_global = cell_rows[2]
    columns_x = jnp.arange(width_x + 16, dtype=jnp.int32) - reach_cells
    columns_y = jnp.arange(width_y + 16, dtype=jnp.int32) - reach_cells
    weight_x = tap_weight(columns_x[None, :] - x_local[:, None])
    weight_y = tap_weight(columns_y[None, :] - y_local[:, None]).astype(jnp.bfloat16)
    every_level = jnp.arange(levels_all, dtype=jnp.int32)
    spread_all = (every_level[None, :] - z_global[:, None]).astype(jnp.float32) / sigma_z
    level_total = jnp.sum(jnp.exp(-spread_all * spread_all), axis=1)
    own_levels = first_level + jnp.arange(levels_here, dtype=jnp.int32)
    spread_own = (own_levels[None, :] - z_global[:, None]).astype(jnp.float32) / sigma_z
    weight_z = jnp.exp(-spread_own * spread_own) / level_total[:, None]
    planes = []
    for channel in range(force_rows.shape[0]):
        weighted = ((force_rows[channel][:, None] * weight_z)[:, :, None] * weight_x[:, None, :]).astype(jnp.bfloat16)
        weighted = weighted.reshape(weighted.shape[0], levels_here * (width_x + 16))
        plane = lax.dot_general(weighted, weight_y, (((0,), (0,)), ((), ())), preferred_element_type=jnp.float32)
        planes.append(plane.reshape(levels_here, width_x + 16, width_y + 16))
    return jnp.stack(planes)


def central_sum(padded):
    along_x = padded[0, 1:-1, 2:, 1:-1] - padded[0, 1:-1, :-2, 1:-1]
    along_y = padded[1, 1:-1, 1:-1, 2:] - padded[1, 1:-1, 1:-1, :-2]
    along_z = padded[2, 2:, 1:-1, 1:-1] - padded[2, :-2, 1:-1, 1:-1]
    return 0.5 * (along_x + along_y + along_z)


def reference(base_state, tendency, inflow, chord_len, twist_base, compliance, blade_frame, owner_tile, point_cells):
    tiles = N_GX * N_GY
    channels = base_state.shape[0]
    forces = point_forces(inflow, chord_len, twist_base, compliance, blade_frame)
    owners = owner_tile[:, 0].reshape(tiles, P_DEV)
    force_blocks = forces.reshape(channels, tiles, P_DEV).transpose(1, 0, 2)
    cell_blocks = point_cells.reshape(3, tiles, P_DEV).transpose(1, 0, 2)

    def pack_block(force_block, cell_block, owner_block):
        return pack_points(force_block, cell_block, owner_block, tiles, CAP)

    force_rows, cell_rows = jax.vmap(pack_block)(force_blocks, cell_blocks, owners)
    tile_force = force_rows.reshape(tiles, channels, tiles, CAP).transpose(2, 1, 0, 3).reshape(tiles, channels, tiles * CAP)
    tile_cells = cell_rows.reshape(tiles, 3, tiles, CAP).transpose(2, 1, 0, 3).reshape(tiles, 3, tiles * CAP)
    canvas_start = jnp.zeros((channels, NZ, NX + 16, NY + 16), jnp.float32)

    def deposit(canvas, inputs):
        tile, one_force, one_cells = inputs
        plane = smear_tile(one_force, one_cells, 0, NZ, NZ, CX, CY)
        start_x = ((tile // N_GY) * CX).astype(jnp.int32)
        start_y = ((tile % N_GY) * CY).astype(jnp.int32)
        anchor = jnp.zeros((), jnp.int32)
        window = lax.dynamic_slice(canvas, (anchor, anchor, start_x, start_y), plane.shape)
        canvas = lax.dynamic_update_slice(canvas, window + plane, (anchor, anchor, start_x, start_y))
        return canvas, None

    canvas, unused = lax.scan(deposit, canvas_start, (jnp.arange(tiles, dtype=jnp.int32), tile_force, tile_cells))
    source = canvas[:, :, 8:-8, 8:-8]
    forced_state = base_state + 0.5 * (tendency.astype(jnp.float32) + source)
    padded = jnp.pad(forced_state[:3], ((0, 0), (1, 1), (1, 1), (1, 1)))
    divergence = central_sum(padded)
    return forced_state, jnp.transpose(divergence, (0, 2, 1))
```

```python
import functools
import math

import jax
import jax.numpy as jnp
from jax import lax
from jax.experimental import pallas as pl
from jax.experimental.pallas import tpu as pltpu
from jax.sharding import PartitionSpec as P

sigma_xy = 3.0
sigma_z = 1.5
reach = 8
tap_total = sum([math.exp(-((float(e) / sigma_xy) ** 2)) for e in range(-8, 9)])
MESH = pl.DeviceIdType.MESH
VM = pl.BlockSpec(memory_space=pltpu.VMEM)
ANY = pl.BlockSpec(memory_space=pl.ANY)
LIMIT = 48 * 1024 * 1024
f32 = jnp.float32
bf16 = jnp.bfloat16


def iota(shape, dim):
    return lax.broadcasted_iota(jnp.int32, shape, dim)


def dot_nt(a, b, precision=None):
    return lax.dot_general(a, b, (((1,), (1,)), ((), ())), precision=precision, preferred_element_type=f32)


def point_forces(inflow, chord_len, twist_base, compliance, blade_frame):
    normal = inflow[0]
    tangent = inflow[1]
    speed_sq = normal * normal + tangent * tangent
    twist_angle = twist_base + compliance * speed_sq
    attack = jnp.arctan2(normal, tangent) - twist_angle
    pressure = 0.5 * speed_sq * chord_len
    lift_force = pressure * (2.0 * math.pi) * jnp.sin(attack)
    drag_force = pressure * (0.01 + 0.5 * attack * attack)
    half = blade_frame.shape[0] // 2
    return blade_frame[:half] * lift_force[None, :] + blade_frame[half:] * drag_force[None, :]


def pack_kernel(tiles, cap, data_ref, owner_ref, out_ref, slot_ref, split_ref, packed_ref):
    points = data_ref.shape[1]
    step = 256
    tri = (iota((step, step), 0) < iota((step, step), 1)).astype(f32).astype(bf16)
    carry = jnp.zeros((tiles, 1), f32)
    for k in range(points // step):
        here = owner_ref[:, k * step : (k + 1) * step]
        hot = (iota((tiles, step), 0) == here).astype(f32)
        rank = jnp.dot(hot.astype(bf16), tri, preferred_element_type=f32)
        position = jnp.sum(hot * (rank + carry), axis=0, keepdims=True)
        carry = carry + jnp.sum(hot, axis=1, keepdims=True)
        slot_ref[:, k * step : (k + 1) * step] = position.astype(jnp.int32) + here * cap
    data = data_ref[...]
    high = data.astype(bf16)
    split_ref[0:16, :] = high
    split_ref[16:32, :] = (data - high.astype(f32)).astype(bf16)
    block = 512
    slots = packed_ref.shape[1]

    def one(j, unused):
        first = pl.multiple_of(j * block, block)
        total = jnp.zeros((32, block), f32)
        part = 768
        for k in range(points // part):
            goal = slot_ref[:, k * part : (k + 1) * part] - first
            hot = jnp.where(iota((block, part), 0) == goal, 1.0, 0.0).astype(bf16)
            total = total + dot_nt(split_ref[:, k * part : (k + 1) * part], hot)
        packed_ref[:, pl.ds(first, block)] = total[0:16] + total[16:32]
        return unused

    lax.fori_loop(0, slots // block, one, 0)
    for t in range(tiles):
        out_ref[t] = packed_ref[:, t * cap : (t + 1) * cap]


def tap_weight(offset):
    scaled = offset.astype(f32) * (1.0 / sigma_xy)
    return jnp.where(jnp.abs(offset) <= reach, jnp.exp(-scaled * scaled) * (1.0 / tap_total), 0.0)


def smear_kernel(
    sources, cap, channels, levels, levels_all, wx, wy, in_ref, center_ref, xs_ref, ys_ref, cn_ref, rows_ref, a_ref, b_ref, h_ref, acc_ref, hacc_ref
):
    px = wx + 16
    slots = sources * cap
    rows_ref[...] = jnp.zeros(rows_ref.shape, f32)
    for s in range(sources):
        rows_ref[:, s * cap : (s + 1) * cap] = in_ref[s]
    first_level = lax.axis_index("gz") * levels
    acc_ref[...] = jnp.zeros(acc_ref.shape, f32)
    hacc_ref[...] = jnp.zeros(hacc_ref.shape, f32)
    chunk = a_ref.shape[1]

    def one(j, unused):
        lanes = pl.ds(pl.multiple_of(j * chunk, chunk), chunk)
        cells = rows_ref[8:16, lanes].astype(jnp.int32)
        x, y, z = cells[0:1], cells[1:2], cells[2:3]
        gx = tap_weight(iota((px, chunk), 0) - reach - x)
        for c in range(channels):
            a_ref[c * px : (c + 1) * px, :] = (rows_ref[c : c + 1, lanes] * gx).astype(bf16)
        every = (iota((levels_all, chunk), 0) - z).astype(f32) * (1.0 / sigma_z)
        total = 1.0 / jnp.sum(jnp.exp(-every * every), axis=0, keepdims=True)
        gy = tap_weight(iota((wy + 16, chunk), 0) - reach - y).astype(bf16).astype(f32)
        for k in range(levels):
            near = (first_level + k - z).astype(f32) * (1.0 / sigma_z)
            gz = jnp.exp(-near * near) * total
            b_ref[k * wy : (k + 1) * wy, :] = (gy[8 : 8 + wy] * gz).astype(bf16)
            rims = jnp.concatenate([gy[0:8] * gz, gy[8 + wy :] * gz], axis=0)
            h_ref[k * 16 : (k + 1) * 16, :] = rims.astype(bf16)
        acc_ref[...] += dot_nt(a_ref[...], b_ref[...])
        hacc_ref[...] += dot_nt(h_ref[...], a_ref[...])
        return unused

    lax.fori_loop(0, rows_ref.shape[1] // chunk, one, 0)
    for c in range(channels):
        center_ref[c] = acc_ref[c * px + 8 : c * px + 8 + wx, :]
        xs_ref[0, c] = acc_ref[c * px : c * px + 8, :]
        xs_ref[1, c] = acc_ref[c * px + 8 + wx : (c + 1) * px, :]
        for k in range(levels):
            for side in range(2):
                rim = hacc_ref[k * 16 + side * 8 : k * 16 + side * 8 + 8, c * px : (c + 1) * px]
                ys_ref[side, c, k * 8 : (k + 1) * 8, :] = rim[:, 8 : 8 + wx]
                cn_ref[side, 0, k * 8 : (k + 1) * 8, c * 8 : (c + 1) * 8] = rim[:, 0:8]
                cn_ref[side, 1, k * 8 : (k + 1) * 8, c * 8 : (c + 1) * 8] = rim[:, 8 + wx :]


def place():
    return (lax.axis_index("group"), lax.axis_index("gx"), lax.axis_index("gy"), lax.axis_index("gz"))


def rim_kernel(nx, ny, xs_ref, ys_ref, cn_ref, rx_ref, ry_ref, rc_ref, send_sem, recv_sem):
    g, x, y, z = place()
    barrier = pltpu.get_barrier_semaphore()
    moves = [(dx, dy) for dx in (-1, 0, 1) for dy in (-1, 0, 1) if (dx, dy) != (0, 0)]

    def there(dx, dy):
        return (x + dx >= 0) & (x + dx < nx) & (y + dy >= 0) & (y + dy < ny)

    def copy(i, dx, dy):
        high_x, high_y = (dx + 1) // 2, (dy + 1) // 2
        if dy == 0:
            src, dst = xs_ref.at[high_x], rx_ref.at[1 - high_x]
        elif dx == 0:
            src, dst = ys_ref.at[high_y], ry_ref.at[1 - high_y]
        else:
            src, dst = cn_ref.at[high_y, high_x], rc_ref.at[1 - high_y, 1 - high_x]
        return pltpu.make_async_remote_copy(
            src_ref=src, dst_ref=dst, send_sem=send_sem.at[i], recv_sem=recv_sem.at[i],
            device_id=(g, x + dx, y + dy, z), device_id_type=MESH,
        )

    count = jnp.int32(0)
    for dx, dy in moves:
        count = count + there(dx, dy).astype(jnp.int32)

        @pl.when(there(dx, dy))
        def _():
            pl.semaphore_signal(barrier, inc=1, device_id=(g, x + dx, y + dy, z), device_id_type=MESH)

    pl.semaphore_wait(barrier, count)
    for i, (dx, dy) in enumerate(moves):

        @pl.when(there(dx, dy))
        def _():
            copy(i, dx, dy).start()

    for i, (dx, dy) in enumerate(moves):

        @pl.when(there(dx, dy))
        def _():
            copy(i, dx, dy).wait_send()

        @pl.when(there(-dx, -dy))
        def _():
            copy(i, dx, dy).wait_recv()


def state_kernel(nx, ny, base_ref, tend_ref, center_ref, rx_ref, ry_ref, rc_ref, out_ref):
    unused_g, x, y, unused_z = place()
    c = pl.program_id(0)
    levels, wx, wy = base_ref.shape[1:]
    low_x, high_x, low_y, high_y = x > 0, x < nx - 1, y > 0, y < ny - 1
    strips = []
    for side, ok_y in ((0, low_y), (1, high_y)):
        strip = jnp.where(ok_y, ry_ref[side, 0], 0.0)
        for end, ok_x in ((0, low_x), (1, high_x)):
            corner = jnp.where(ok_y & ok_x, rc_ref[side, end], 0.0)
            size = corner.shape[1]
            row, col = iota((size, wx), 0), iota((size, wx), 1)
            put = ((row - c * 8 == col - end * (wx - 8)) & (row >= c * 8) & (row < c * 8 + 8)).astype(f32)
            strip = strip + jnp.dot(corner, put, precision=lax.Precision.HIGHEST, preferred_element_type=f32)
        strips.append(strip)
    strip = jnp.concatenate(strips, axis=0)
    half = levels * 8
    row, col = iota((2 * half, levels * wy), 0), iota((2 * half, levels * wy), 1)
    side, level, cell = row // half, (row % half) // 8, row % 8
    put = (col == level * wy + cell + side * (wy - 8)).astype(f32)
    source = center_ref[0] + lax.dot_general(
        strip, put, (((0,), (0,)), ((), ())), precision=lax.Precision.HIGHEST, preferred_element_type=f32
    )
    source = jnp.concatenate(
        [
            source[:8] + jnp.where(low_x, rx_ref[0, 0], 0.0),
            source[8:-8],
            source[-8:] + jnp.where(high_x, rx_ref[1, 0], 0.0),
        ],
        axis=0,
    )
    for k in range(levels):
        out_ref[0, k] = base_ref[0, k] + 0.5 * (tend_ref[0, k].astype(f32) + source[:, k * wy : (k + 1) * wy])


def lines_kernel(nx, ny, nz, fs_ref, out_ref, su, sv, ru, rv, rw, lines, land, hs, hr, ls, lr):
    g, x, y, z = place()
    unused, levels, wx, wy = fs_ref.shape
    barrier = pltpu.get_barrier_semaphore()

    def at(axis, d):
        return (g, x + d if axis == 0 else x, y + d if axis == 1 else y, z + d if axis == 2 else z)

    def there(axis, d):
        here, count = ((x, nx), (y, ny), (z, nz))[axis]
        return (here + d >= 0) & (here + d < count)

    for k in range(1, nx):
        pl.semaphore_signal(barrier, inc=1, device_id=(g, lax.rem(x + k, nx), y, z), device_id_type=MESH)
    count = jnp.int32(nx - 1)
    for axis in (1, 2):
        for d in (-1, 1):
            count = count + there(axis, d).astype(jnp.int32)

            @pl.when(there(axis, d))
            def _():
                pl.semaphore_signal(barrier, inc=1, device_id=at(axis, d), device_id_type=MESH)

    across = [jnp.transpose(fs_ref[1, k]) for k in range(levels)]
    for k in range(levels):
        su[0, k : k + 1, :] = fs_ref[0, k, 0:1, :]
        su[1, k : k + 1, :] = fs_ref[0, k, wx - 1 : wx, :]
        sv[0, k : k + 1, :] = across[k][0:1]
        sv[1, k : k + 1, :] = across[k][wy - 1 : wy]
    pl.semaphore_wait(barrier, count)

    def halo(axis, d):
        i = axis * 2 + (d + 1) // 2
        high = (d + 1) // 2
        if axis == 0:
            src, dst = su.at[high], ru.at[1 - high]
        elif axis == 1:
            src, dst = sv.at[high], rv.at[1 - high]
        else:
            src, dst = fs_ref.at[2, (levels - 1) * high], rw.at[1 - high]
        return pltpu.make_async_remote_copy(
            src_ref=src, dst_ref=dst, send_sem=hs.at[i], recv_sem=hr.at[i], device_id=at(axis, d), device_id_type=MESH
        )

    moves = [(axis, d) for axis in range(3) for d in (-1, 1)]
    for axis, d in moves:

        @pl.when(there(axis, d))
        def _():
            halo(axis, d).start()

        @pl.when(jnp.logical_not(there(axis, d)))
        def _():
            into = (ru, rv, rw)[axis]
            into[(d + 1) // 2] = jnp.zeros(into.shape[1:], f32)

    for axis, d in moves:

        @pl.when(there(axis, d))
        def _():
            halo(axis, d).wait_send()

        @pl.when(there(axis, -d))
        def _():
            halo(axis, d).wait_recv()

    band = wy // nx
    for k in range(levels):
        u = fs_ref[0, k]
        along = jnp.concatenate([u[1:], ru[1, k : k + 1, :]], axis=0) - jnp.concatenate([ru[0, k : k + 1, :], u[:-1]], axis=0)
        above = fs_ref[2, k + 1] if k + 1 < levels else rw[1]
        below = fs_ref[2, k - 1] if k > 0 else rw[0]
        v = across[k]
        over = jnp.concatenate([v[1:], rv[1, k : k + 1, :]], axis=0) - jnp.concatenate([rv[0, k : k + 1, :], v[:-1]], axis=0)
        div = 0.5 * (jnp.transpose(along + (above - below)) + over)
        for j in range(nx):
            lines[j, k] = div[j * band : (j + 1) * band]

    def line(k):
        far = lax.rem(x + k, nx)
        return pltpu.make_async_remote_copy(
            src_ref=lines.at[far], dst_ref=land.at[x], send_sem=ls.at[k], recv_sem=lr.at[k],
            device_id=(g, far, y, z), device_id_type=MESH,
        )

    def arrival(k):
        far = lax.rem(x + nx - k, nx)
        return pltpu.make_async_remote_copy(
            src_ref=lines.at[far], dst_ref=land.at[far], send_sem=ls.at[k], recv_sem=lr.at[k],
            device_id=(g, far, y, z), device_id_type=MESH,
        )

    for k in range(1, nx):
        line(k).start()
    land[x] = lines[x]
    for k in range(1, nx):
        line(k).wait_send()
        arrival(k).wait_recv()
    for j in range(nx):
        out_ref[:, :, j * wx : (j + 1) * wx] = land[j]


def params(collective_id=None):
    if collective_id is None:
        return pltpu.CompilerParams(vmem_limit_bytes=LIMIT)
    return pltpu.CompilerParams(vmem_limit_bytes=LIMIT, collective_id=collective_id, has_side_effects=True)


def body(base_state, tendency, inflow, chord_len, twist_base, compliance, blade_frame, owner_tile, point_cells):
    nx, ny, nz = lax.axis_size("gx"), lax.axis_size("gy"), lax.axis_size("gz")
    tiles = nx * ny
    points = owner_tile.shape[0]
    cap = max(2, (2 * points + tiles - 1) // tiles)
    channels, levels, wx, wy = base_state.shape
    px = wx + 16
    forces = point_forces(inflow, chord_len, twist_base, compliance, blade_frame)
    data = jnp.concatenate([forces, point_cells.astype(f32), jnp.zeros((5, points), f32)], axis=0)
    slots = -(-tiles * cap // 512) * 512
    shape = jax.ShapeDtypeStruct
    packed = pl.pallas_call(
        functools.partial(pack_kernel, tiles, cap),
        out_shape=shape((tiles, 16, cap), f32),
        in_specs=[VM, VM],
        out_specs=VM,
        scratch_shapes=[pltpu.VMEM((1, points), jnp.int32), pltpu.VMEM((32, points), bf16), pltpu.VMEM((16, slots), f32)],
        compiler_params=params(),
        name="pack_points",
    )(data, owner_tile.reshape(1, points))
    arrived = lax.all_to_all(packed, ("gx", "gy"), split_axis=0, concat_axis=0, tiled=True)
    chunk = 512
    center, xs, ys, cn = pl.pallas_call(
        functools.partial(smear_kernel, tiles, cap, channels, levels, levels * nz, wx, wy),
        out_shape=(
            shape((channels, wx, levels * wy), f32),
            shape((2, channels, 8, levels * wy), f32),
            shape((2, channels, levels * 8, wx), f32),
            shape((2, 2, levels * 8, channels * 8), f32),
        ),
        in_specs=[VM],
        out_specs=(VM,) * 4,
        scratch_shapes=[
            pltpu.VMEM((16, slots), f32),
            pltpu.VMEM((channels * px, chunk), bf16),
            pltpu.VMEM((levels * wy, chunk), bf16),
            pltpu.VMEM((levels * 16, chunk), bf16),
            pltpu.VMEM((channels * px, levels * wy), f32),
            pltpu.VMEM((levels * 16, channels * px), f32),
        ],
        compiler_params=params(),
        name="smear_points",
    )(arrived)
    rx, ry, rc = pl.pallas_call(
        functools.partial(rim_kernel, nx, ny),
        out_shape=(shape(xs.shape, f32), shape(ys.shape, f32), shape(cn.shape, f32)),
        in_specs=[ANY] * 3,
        out_specs=(ANY,) * 3,
        scratch_shapes=[pltpu.SemaphoreType.DMA((8,)), pltpu.SemaphoreType.DMA((8,))],
        compiler_params=params(1),
        name="exchange_rims",
    )(xs, ys, cn)
    forced_state = pl.pallas_call(
        functools.partial(state_kernel, nx, ny),
        grid=(channels,),
        out_shape=shape(base_state.shape, f32),
        in_specs=[
            pl.BlockSpec((1, levels, wx, wy), lambda c: (c, 0, 0, 0)),
            pl.BlockSpec((1, levels, wx, wy), lambda c: (c, 0, 0, 0)),
            pl.BlockSpec((1, wx, levels * wy), lambda c: (c, 0, 0)),
            pl.BlockSpec((2, 1, 8, levels * wy), lambda c: (0, c, 0, 0)),
            pl.BlockSpec((2, 1, levels * 8, wx), lambda c: (0, c, 0, 0)),
            pl.BlockSpec(cn.shape, lambda c: (0, 0, 0, 0)),
        ],
        out_specs=pl.BlockSpec((1, levels, wx, wy), lambda c: (c, 0, 0, 0)),
        compiler_params=params(),
        name="forced_state",
    )(base_state, tendency, center, rx, ry, rc)
    band = wy // nx
    divergence_lines = pl.pallas_call(
        functools.partial(lines_kernel, nx, ny, nz),
        grid=(1,),
        out_shape=shape((levels, band, nx * wx), f32),
        in_specs=[pl.BlockSpec((3, levels, wx, wy), lambda i: (0, 0, 0, 0))],
        out_specs=pl.BlockSpec((levels, band, nx * wx), lambda i: (0, 0, 0)),
        scratch_shapes=[
            pltpu.VMEM((2, levels, wy), f32),
            pltpu.VMEM((2, levels, wx), f32),
            pltpu.VMEM((2, levels, wy), f32),
            pltpu.VMEM((2, levels, wx), f32),
            pltpu.VMEM((2, wx, wy), f32),
            pltpu.VMEM((nx, levels, band, wx), f32),
            pltpu.VMEM((nx, levels, band, wx), f32),
            pltpu.SemaphoreType.DMA((6,)),
            pltpu.SemaphoreType.DMA((6,)),
            pltpu.SemaphoreType.DMA((nx,)),
            pltpu.SemaphoreType.DMA((nx,)),
        ],
        compiler_params=params(2),
        name="divergence_lines",
    )(forced_state)
    return (forced_state, divergence_lines)


def solution(mesh):
    in_specs = (
        P("group", "gz", "gx", "gy"),
        P("group", "gz", "gx", "gy"),
        P("group", ("gx", "gy")),
        P(("group", "gx", "gy")),
        P(("group", "gx", "gy")),
        P(("group", "gx", "gy")),
        P("group", ("gx", "gy")),
        P(("gx", "gy"), "group"),
        P("group", ("gx", "gy")),
    )
    out_specs = (P("group", "gz", "gx", "gy"), P(("group", "gz"), ("gy", "gx"), None))
    return jax.shard_map(body, mesh=mesh, in_specs=in_specs, out_specs=out_specs, check_vma=False)
```

```python
import functools
import math

import jax
import jax.numpy as jnp
from jax import lax
from jax.experimental import pallas as pl
from jax.experimental.pallas import tpu as pltpu
from jax.sharding import PartitionSpec as P

sigma_xy = 3.0
sigma_z = 1.5
reach = 8
tap_total = sum([math.exp(-((float(e) / sigma_xy) ** 2)) for e in range(-8, 9)])
MESH = pl.DeviceIdType.MESH
VM = pl.BlockSpec(memory_space=pltpu.VMEM)
ANY = pl.BlockSpec(memory_space=pl.ANY)
LIMIT = 48 * 1024 * 1024
f32 = jnp.float32
bf16 = jnp.bfloat16


def iota(shape, dim):
    return lax.broadcasted_iota(jnp.int32, shape, dim)


def dot_nt(a, b, precision=None):
    return lax.dot_general(a, b, (((1,), (1,)), ((), ())), precision=precision, preferred_element_type=f32)


def arc_tangent(n, t):
    small, large = jnp.minimum(n, t), jnp.maximum(n, t)
    upper = small > 0.41421356 * large
    r = jnp.where(upper, small - large, small) / jnp.where(upper, small + large, large)
    q = r * r
    poly = ((8.05374449538e-2 * q - 1.38776856032e-1) * q + 1.99777106478e-1) * q - 3.33329491539e-1
    angle = jnp.where(upper, math.pi / 4, 0.0) + (poly * q * r + r)
    return jnp.where(n > t, math.pi / 2 - angle, angle)


def pack_kernel(
    tiles, cap, half, inflow_ref, chord_ref, twist_ref, compliance_ref, frame_ref, owner_ref, cells_ref, out_ref, slot_ref, split_ref, packed_ref
):
    points = owner_ref.shape[1]
    step = 256
    tri = (iota((step, step), 0) < iota((step, step), 1)).astype(f32).astype(bf16)
    carry = jnp.zeros((tiles, 1), f32)
    mine = lax.axis_index("gz") * half
    wide = -(-cap // 128) * 128
    for k in range(points // step):
        here = owner_ref[:, k * step : (k + 1) * step]
        hot = (iota((tiles, step), 0) == here).astype(f32)
        rank = jnp.dot(hot.astype(bf16), tri, preferred_element_type=f32)
        position = jnp.sum(hot * (rank + carry), axis=0, keepdims=True)
        carry = carry + jnp.sum(hot, axis=1, keepdims=True)
        slot_ref[:, k * step : (k + 1) * step] = position.astype(jnp.int32) + (here - mine) * wide
    normal, tangent = inflow_ref[0:1, :], inflow_ref[1:2, :]
    speed_sq = normal * normal + tangent * tangent
    attack = arc_tangent(normal, tangent) - (twist_ref[...] + compliance_ref[...] * speed_sq)
    pressure = 0.5 * speed_sq * chord_ref[...]
    lift = pressure * (2.0 * math.pi) * jnp.sin(attack)
    drag = pressure * (0.01 + 0.5 * attack * attack)
    channels = frame_ref.shape[0] // 2
    forces = frame_ref[:channels, :] * lift + frame_ref[channels:, :] * drag
    high = forces.astype(bf16).astype(f32)
    cells = jnp.concatenate([cells_ref[...].astype(f32), jnp.zeros((13, points), f32)], axis=0)
    split_ref[0:16, :] = jnp.concatenate([high, forces - high], axis=0).astype(bf16)
    split_ref[16:32, :] = cells.astype(bf16)
    block = 512
    slots = packed_ref.shape[1]

    def one(j, unused):
        first = pl.multiple_of(j * block, block)
        total = jnp.zeros((32, block), f32)
        part = 768
        for k in range(points // part):
            goal = slot_ref[:, k * part : (k + 1) * part] - first
            hot = jnp.where(iota((block, part), 0) == goal, 1.0, 0.0).astype(bf16)
            total = total + dot_nt(split_ref[:, k * part : (k + 1) * part], hot)
        packed_ref[0:8, pl.ds(first, block)] = total[0:8] + total[8:16]
        packed_ref[8:16, pl.ds(first, block)] = total[16:24]
        return unused

    lax.fori_loop(0, slots // block, one, 0)
    pieces = wide // 128
    for t in range(half):
        out_ref[t] = jnp.zeros(out_ref.shape[1:], f32)
        out_ref[t, :, 0:wide] = packed_ref[0:8, t * wide : (t + 1) * wide]
        for i in range(3):
            for j in range(pieces):
                row = i * pieces + j
                out_ref[t, row % 8 : row % 8 + 1, wide + row // 8 * 128 : wide + row // 8 * 128 + 128] = packed_ref[
                    8 + i : 9 + i, t * wide + j * 128 : t * wide + (j + 1) * 128
                ]


def points_kernel(tiles, cap, half, ny, in_ref, out_ref, land, send_sem, recv_sem, out_sem, pass_sem):
    g, x, y, z = place()
    me = x * ny + y
    owns = me // half == z
    barrier = pltpu.get_barrier_semaphore()

    def device(t):
        return (g, t // ny, t % ny, z)

    sibling = (g, x, y, 1 - z)

    @pl.when(owns)
    def _():
        def greet(k, unused):
            pl.semaphore_signal(barrier, inc=1, device_id=device(lax.rem(me + k, tiles)), device_id_type=MESH)
            return unused

        lax.fori_loop(1, tiles, greet, 0)

    pl.semaphore_signal(barrier, inc=1, device_id=sibling, device_id_type=MESH)
    pl.semaphore_wait(barrier, half + 1 - owns.astype(jnp.int32))

    def send(k):
        far = z * half + lax.rem(me + k, half)
        return far, pltpu.make_async_remote_copy(
            src_ref=in_ref.at[far - z * half], dst_ref=land.at[me], send_sem=send_sem.at[k], recv_sem=recv_sem.at[me],
            device_id=device(far), device_id_type=MESH,
        )

    def hand(s):
        return pltpu.make_async_remote_copy(
            src_ref=land.at[s], dst_ref=land.at[s], send_sem=out_sem.at[s], recv_sem=pass_sem.at[s],
            device_id=sibling, device_id_type=MESH,
        )

    def start(k, unused):
        far, copy = send(k)

        @pl.when(far != me)
        def _():
            copy.start()

        return unused

    lax.fori_loop(0, half, start, 0)

    @pl.when(owns)
    def _():
        land[me] = in_ref[me - z * half]
        hand(me).start()

        def take(k, unused):
            s = lax.rem(me + k, tiles)
            pltpu.make_async_remote_copy(
                src_ref=in_ref.at[0], dst_ref=land.at[s], send_sem=send_sem.at[0], recv_sem=recv_sem.at[s],
                device_id=device(s), device_id_type=MESH,
            ).wait_recv()
            hand(s).start()
            return unused

        lax.fori_loop(1, tiles, take, 0)

        def sent(s, unused):
            hand(s).wait_send()
            return unused

        lax.fori_loop(0, tiles, sent, 0)

    @pl.when(jnp.logical_not(owns))
    def _():
        def got(s, unused):
            hand(s).wait_recv()
            return unused

        lax.fori_loop(0, tiles, got, 0)

    def finish(k, unused):
        far, copy = send(k)

        @pl.when(far != me)
        def _():
            copy.wait_send()

        return unused

    lax.fori_loop(0, half, finish, 0)
    wide = -(-cap // 128) * 128
    pieces = wide // 128
    if out_ref.shape[1] > tiles * cap:
        out_ref[...] = jnp.zeros(out_ref.shape, f32)
    for s in range(tiles):
        out_ref[0:8, s * cap : (s + 1) * cap] = land[s, :, 0:cap]
        for i in range(3):
            for j in range(pieces):
                row = i * pieces + j
                size = min(128, cap - j * 128)
                out_ref[8 + i : 9 + i, s * cap + j * 128 : s * cap + j * 128 + size] = land[
                    s, row % 8 : row % 8 + 1, wide + row // 8 * 128 : wide + row // 8 * 128 + size
                ]


def tap_weight(offset):
    scaled = offset.astype(f32) * (1.0 / sigma_xy)
    return jnp.where(jnp.abs(offset) <= reach, jnp.exp(-scaled * scaled) * (1.0 / tap_total), 0.0)


def smear_kernel(
    sources, cap, channels, levels, levels_all, wx, wy, rows_ref, center_ref, xs_ref, ys_ref, cn_ref, a_ref, b_ref, h_ref, acc_ref, hacc_ref
):
    px = wx + 16
    first_level = lax.axis_index("gz") * levels
    acc_ref[...] = jnp.zeros(acc_ref.shape, f32)
    hacc_ref[...] = jnp.zeros(hacc_ref.shape, f32)
    chunk = a_ref.shape[1]

    def one(j, unused):
        lanes = pl.ds(pl.multiple_of(j * chunk, chunk), chunk)
        cells = rows_ref[8:11, lanes].astype(jnp.int32)
        x, y, z = cells[0:1], cells[1:2], cells[2:3]
        gx = tap_weight(iota((px, chunk), 0) - reach - x)
        for c in range(channels):
            a_ref[c * px : (c + 1) * px, :] = (rows_ref[c : c + 1, lanes] * gx).astype(bf16)
        every = (iota((levels_all, chunk), 0) - z).astype(f32) * (1.0 / sigma_z)
        total = 1.0 / jnp.sum(jnp.exp(-every * every), axis=0, keepdims=True)
        gy = tap_weight(iota((wy + 16, chunk), 0) - reach - y).astype(bf16).astype(f32)
        for k in range(levels):
            near = (first_level + k - z).astype(f32) * (1.0 / sigma_z)
            gz = jnp.exp(-near * near) * total
            b_ref[k * wy : (k + 1) * wy, :] = (gy[8 : 8 + wy] * gz).astype(bf16)
            rims = jnp.concatenate([gy[0:8] * gz, gy[8 + wy :] * gz], axis=0)
            h_ref[k * 16 : (k + 1) * 16, :] = rims.astype(bf16)
        acc_ref[...] += dot_nt(a_ref[...], b_ref[...])
        hacc_ref[...] += dot_nt(h_ref[...], a_ref[...])
        return unused

    lax.fori_loop(0, rows_ref.shape[1] // chunk, one, 0)
    for c in range(channels):
        center_ref[c] = acc_ref[c * px + 8 : c * px + 8 + wx, :]
        xs_ref[0, c] = acc_ref[c * px : c * px + 8, :]
        xs_ref[1, c] = acc_ref[c * px + 8 + wx : (c + 1) * px, :]
        for k in range(levels):
            for side in range(2):
                rim = hacc_ref[k * 16 + side * 8 : k * 16 + side * 8 + 8, c * px : (c + 1) * px]
                ys_ref[side, c, k * 8 : (k + 1) * 8, :] = rim[:, 8 : 8 + wx]
                cn_ref[side, 0, k * 8 : (k + 1) * 8, c * 8 : (c + 1) * 8] = rim[:, 0:8]
                cn_ref[side, 1, k * 8 : (k + 1) * 8, c * 8 : (c + 1) * 8] = rim[:, 8 + wx :]


def place():
    return (lax.axis_index("group"), lax.axis_index("gx"), lax.axis_index("gy"), lax.axis_index("gz"))


def rim_kernel(nx, ny, xs_ref, ys_ref, cn_ref, rx_ref, ry_ref, rc_ref, send_sem, recv_sem):
    g, x, y, z = place()
    barrier = pltpu.get_barrier_semaphore()
    moves = [(dx, dy) for dx in (-1, 0, 1) for dy in (-1, 0, 1) if (dx, dy) != (0, 0)]

    def there(dx, dy):
        return (x + dx >= 0) & (x + dx < nx) & (y + dy >= 0) & (y + dy < ny)

    def copy(i, dx, dy):
        high_x, high_y = (dx + 1) // 2, (dy + 1) // 2
        if dy == 0:
            src, dst = xs_ref.at[high_x], rx_ref.at[1 - high_x]
        elif dx == 0:
            src, dst = ys_ref.at[high_y], ry_ref.at[1 - high_y]
        else:
            src, dst = cn_ref.at[high_y, high_x], rc_ref.at[1 - high_y, 1 - high_x]
        return pltpu.make_async_remote_copy(
            src_ref=src, dst_ref=dst, send_sem=send_sem.at[i], recv_sem=recv_sem.at[i],
            device_id=(g, x + dx, y + dy, z), device_id_type=MESH,
        )

    count = jnp.int32(0)
    for dx, dy in moves:
        count = count + there(dx, dy).astype(jnp.int32)

        @pl.when(there(dx, dy))
        def _():
            pl.semaphore_signal(barrier, inc=1, device_id=(g, x + dx, y + dy, z), device_id_type=MESH)

    pl.semaphore_wait(barrier, count)
    for i, (dx, dy) in enumerate(moves):

        @pl.when(there(dx, dy))
        def _():
            copy(i, dx, dy).start()

    for i, (dx, dy) in enumerate(moves):

        @pl.when(there(dx, dy))
        def _():
            copy(i, dx, dy).wait_send()

        @pl.when(there(-dx, -dy))
        def _():
            copy(i, dx, dy).wait_recv()


def two(value, axis):
    high = value.astype(bf16)
    return jnp.concatenate([high, (value - high.astype(f32)).astype(bf16)], axis=axis)


def state_kernel(nx, ny, base_ref, tend_ref, center_ref, rx_ref, ry_ref, rc_ref, out_ref):
    unused_g, x, y, unused_z = place()
    c = pl.program_id(0)
    levels, wx, wy = base_ref.shape[1:]
    low_x, high_x, low_y, high_y = x > 0, x < nx - 1, y > 0, y < ny - 1
    strips = []
    for side, ok_y in ((0, low_y), (1, high_y)):
        strip = jnp.where(ok_y, ry_ref[side, 0], 0.0)
        for end, ok_x in ((0, low_x), (1, high_x)):
            corner = jnp.where(ok_y & ok_x, rc_ref[side, end], 0.0)
            size = corner.shape[1]
            row, col = iota((size, wx), 0), iota((size, wx), 1)
            put = ((row - c * 8 == col - end * (wx - 8)) & (row >= c * 8) & (row < c * 8 + 8)).astype(f32)
            strip = strip + jnp.dot(two(corner, 1), jnp.concatenate([put, put], axis=0).astype(bf16), preferred_element_type=f32)
        strips.append(strip)
    strip = jnp.concatenate(strips, axis=0)
    half = levels * 8
    row, col = iota((2 * half, levels * wy), 0), iota((2 * half, levels * wy), 1)
    side, level, cell = row // half, (row % half) // 8, row % 8
    put = (col == level * wy + cell + side * (wy - 8)).astype(f32)
    put = jnp.concatenate([put, put], axis=0).astype(bf16)
    source = center_ref[0] + lax.dot_general(two(strip, 0), put, (((0,), (0,)), ((), ())), preferred_element_type=f32)
    source = jnp.concatenate(
        [
            source[:8] + jnp.where(low_x, rx_ref[0, 0], 0.0),
            source[8:-8],
            source[-8:] + jnp.where(high_x, rx_ref[1, 0], 0.0),
        ],
        axis=0,
    )
    for k in range(levels):
        out_ref[0, k] = base_ref[0, k] + 0.5 * (tend_ref[0, k].astype(f32) + source[:, k * wy : (k + 1) * wy])


def lines_kernel(nx, ny, nz, fs_ref, out_ref, su, sv, ru, rv, rw, lines, land, hs, hr, ls, lr):
    g, x, y, z = place()
    unused, levels, wx, wy = fs_ref.shape
    barrier = pltpu.get_barrier_semaphore()

    def at(axis, d):
        return (g, x + d if axis == 0 else x, y + d if axis == 1 else y, z + d if axis == 2 else z)

    def there(axis, d):
        here, count = ((x, nx), (y, ny), (z, nz))[axis]
        return (here + d >= 0) & (here + d < count)

    for k in range(1, nx):
        pl.semaphore_signal(barrier, inc=1, device_id=(g, lax.rem(x + k, nx), y, z), device_id_type=MESH)
    count = jnp.int32(nx - 1)
    for axis in (1, 2):
        for d in (-1, 1):
            count = count + there(axis, d).astype(jnp.int32)

            @pl.when(there(axis, d))
            def _():
                pl.semaphore_signal(barrier, inc=1, device_id=at(axis, d), device_id_type=MESH)

    across = [jnp.transpose(fs_ref[1, k]) for k in range(levels)]
    for k in range(levels):
        su[0, k : k + 1, :] = fs_ref[0, k, 0:1, :]
        su[1, k : k + 1, :] = fs_ref[0, k, wx - 1 : wx, :]
        sv[0, k : k + 1, :] = across[k][0:1]
        sv[1, k : k + 1, :] = across[k][wy - 1 : wy]
    pl.semaphore_wait(barrier, count)

    def halo(axis, d):
        i = axis * 2 + (d + 1) // 2
        high = (d + 1) // 2
        if axis == 0:
            src, dst = su.at[high], ru.at[1 - high]
        elif axis == 1:
            src, dst = sv.at[high], rv.at[1 - high]
        else:
            src, dst = fs_ref.at[2, (levels - 1) * high], rw.at[1 - high]
        return pltpu.make_async_remote_copy(
            src_ref=src, dst_ref=dst, send_sem=hs.at[i], recv_sem=hr.at[i], device_id=at(axis, d), device_id_type=MESH
        )

    moves = [(axis, d) for axis in range(3) for d in (-1, 1)]
    for axis, d in moves:

        @pl.when(there(axis, d))
        def _():
            halo(axis, d).start()

        @pl.when(jnp.logical_not(there(axis, d)))
        def _():
            into = (ru, rv, rw)[axis]
            into[(d + 1) // 2] = jnp.zeros(into.shape[1:], f32)

    for axis, d in moves:

        @pl.when(there(axis, d))
        def _():
            halo(axis, d).wait_send()

        @pl.when(there(axis, -d))
        def _():
            halo(axis, d).wait_recv()

    band = wy // nx
    for k in range(levels):
        u = fs_ref[0, k]
        along = jnp.concatenate([u[1:], ru[1, k : k + 1, :]], axis=0) - jnp.concatenate([ru[0, k : k + 1, :], u[:-1]], axis=0)
        above = fs_ref[2, k + 1] if k + 1 < levels else rw[1]
        below = fs_ref[2, k - 1] if k > 0 else rw[0]
        v = across[k]
        over = jnp.concatenate([v[1:], rv[1, k : k + 1, :]], axis=0) - jnp.concatenate([rv[0, k : k + 1, :], v[:-1]], axis=0)
        div = 0.5 * (jnp.transpose(along + (above - below)) + over)
        for j in range(nx):
            lines[j, k] = div[j * band : (j + 1) * band]

    def line(k):
        far = lax.rem(x + k, nx)
        return pltpu.make_async_remote_copy(
            src_ref=lines.at[far], dst_ref=land.at[x], send_sem=ls.at[k], recv_sem=lr.at[k],
            device_id=(g, far, y, z), device_id_type=MESH,
        )

    def arrival(k):
        far = lax.rem(x + nx - k, nx)
        return pltpu.make_async_remote_copy(
            src_ref=lines.at[far], dst_ref=land.at[far], send_sem=ls.at[k], recv_sem=lr.at[k],
            device_id=(g, far, y, z), device_id_type=MESH,
        )

    for k in range(1, nx):
        line(k).start()
    land[x] = lines[x]
    for k in range(1, nx):
        line(k).wait_send()
        arrival(k).wait_recv()
    for j in range(nx):
        out_ref[:, :, j * wx : (j + 1) * wx] = land[j]


def params(collective_id=None):
    if collective_id is None:
        return pltpu.CompilerParams(vmem_limit_bytes=LIMIT)
    return pltpu.CompilerParams(vmem_limit_bytes=LIMIT, collective_id=collective_id, has_side_effects=True)


def body(base_state, tendency, inflow, chord_len, twist_base, compliance, blade_frame, owner_tile, point_cells):
    nx, ny, nz = lax.axis_size("gx"), lax.axis_size("gy"), lax.axis_size("gz")
    tiles = nx * ny
    points = owner_tile.shape[0]
    cap = max(2, (2 * points + tiles - 1) // tiles)
    channels, levels, wx, wy = base_state.shape
    px = wx + 16
    half = tiles // nz
    wide = -(-cap // 128) * 128
    slots = -(-tiles * cap // 512) * 512
    message = wide + -(-3 * (wide // 128) // 8) * 128
    shape = jax.ShapeDtypeStruct
    packed = pl.pallas_call(
        functools.partial(pack_kernel, tiles, cap, half),
        out_shape=shape((half, 8, message), f32),
        in_specs=[VM] * 7,
        out_specs=VM,
        scratch_shapes=[
            pltpu.VMEM((1, points), jnp.int32),
            pltpu.VMEM((32, points), bf16),
            pltpu.VMEM((16, -(-half * wide // 512) * 512), f32),
        ],
        compiler_params=params(),
        name="pack_points",
    )(
        inflow,
        chord_len.reshape(1, points),
        twist_base.reshape(1, points),
        compliance.reshape(1, points),
        blade_frame,
        owner_tile.reshape(1, points),
        point_cells,
    )
    arrived = pl.pallas_call(
        functools.partial(points_kernel, tiles, cap, half, ny),
        out_shape=shape((16, slots), f32),
        in_specs=[VM],
        out_specs=VM,
        scratch_shapes=[
            pltpu.VMEM((tiles, 8, message), f32),
            pltpu.SemaphoreType.DMA((half,)),
            pltpu.SemaphoreType.DMA((tiles,)),
            pltpu.SemaphoreType.DMA((tiles,)),
            pltpu.SemaphoreType.DMA((tiles,)),
        ],
        compiler_params=params(0),
        name="exchange_points",
    )(packed)
    chunk = 512
    center, xs, ys, cn = pl.pallas_call(
        functools.partial(smear_kernel, tiles, cap, channels, levels, levels * nz, wx, wy),
        out_shape=(
            shape((channels, wx, levels * wy), f32),
            shape((2, channels, 8, levels * wy), f32),
            shape((2, channels, levels * 8, wx), f32),
            shape((2, 2, levels * 8, channels * 8), f32),
        ),
        in_specs=[VM],
        out_specs=(VM,) * 4,
        scratch_shapes=[
            pltpu.VMEM((channels * px, chunk), bf16),
            pltpu.VMEM((levels * wy, chunk), bf16),
            pltpu.VMEM((levels * 16, chunk), bf16),
            pltpu.VMEM((channels * px, levels * wy), f32),
            pltpu.VMEM((levels * 16, channels * px), f32),
        ],
        compiler_params=params(),
        name="smear_points",
    )(arrived)
    rx, ry, rc = pl.pallas_call(
        functools.partial(rim_kernel, nx, ny),
        out_shape=(shape(xs.shape, f32), shape(ys.shape, f32), shape(cn.shape, f32)),
        in_specs=[ANY] * 3,
        out_specs=(ANY,) * 3,
        scratch_shapes=[pltpu.SemaphoreType.DMA((8,)), pltpu.SemaphoreType.DMA((8,))],
        compiler_params=params(1),
        name="exchange_rims",
    )(xs, ys, cn)
    forced_state = pl.pallas_call(
        functools.partial(state_kernel, nx, ny),
        grid=(channels,),
        out_shape=shape(base_state.shape, f32),
        in_specs=[
            pl.BlockSpec((1, levels, wx, wy), lambda c: (c, 0, 0, 0)),
            pl.BlockSpec((1, levels, wx, wy), lambda c: (c, 0, 0, 0)),
            pl.BlockSpec((1, wx, levels * wy), lambda c: (c, 0, 0)),
            pl.BlockSpec((2, 1, 8, levels * wy), lambda c: (0, c, 0, 0)),
            pl.BlockSpec((2, 1, levels * 8, wx), lambda c: (0, c, 0, 0)),
            pl.BlockSpec(cn.shape, lambda c: (0, 0, 0, 0)),
        ],
        out_specs=pl.BlockSpec((1, levels, wx, wy), lambda c: (c, 0, 0, 0)),
        compiler_params=params(),
        name="forced_state",
    )(base_state, tendency, center, rx, ry, rc)
    band = wy // nx
    divergence_lines = pl.pallas_call(
        functools.partial(lines_kernel, nx, ny, nz),
        grid=(1,),
        out_shape=shape((levels, band, nx * wx), f32),
        in_specs=[pl.BlockSpec((3, levels, wx, wy), lambda i: (0, 0, 0, 0))],
        out_specs=pl.BlockSpec((levels, band, nx * wx), lambda i: (0, 0, 0)),
        scratch_shapes=[
            pltpu.VMEM((2, levels, wy), f32),
            pltpu.VMEM((2, levels, wx), f32),
            pltpu.VMEM((2, levels, wy), f32),
            pltpu.VMEM((2, levels, wx), f32),
            pltpu.VMEM((2, wx, wy), f32),
            pltpu.VMEM((nx, levels, band, wx), f32),
            pltpu.VMEM((nx, levels, band, wx), f32),
            pltpu.SemaphoreType.DMA((6,)),
            pltpu.SemaphoreType.DMA((6,)),
            pltpu.SemaphoreType.DMA((nx,)),
            pltpu.SemaphoreType.DMA((nx,)),
        ],
        compiler_params=params(2),
        name="divergence_lines",
    )(forced_state)
    return (forced_state, divergence_lines)


def solution(mesh):
    in_specs = (
        P("group", "gz", "gx", "gy"),
        P("group", "gz", "gx", "gy"),
        P("group", ("gx", "gy")),
        P(("group", "gx", "gy")),
        P(("group", "gx", "gy")),
        P(("group", "gx", "gy")),
        P("group", ("gx", "gy")),
        P(("gx", "gy"), "group"),
        P("group", ("gx", "gy")),
    )
    out_specs = (P("group", "gz", "gx", "gy"), P(("group", "gz"), ("gy", "gx"), None))
    return jax.shard_map(body, mesh=mesh, in_specs=in_specs, out_specs=out_specs, check_vma=False)
```

```python
import functools
import math

import jax
import jax.numpy as jnp
from jax import lax
from jax.experimental import pallas as pl
from jax.experimental.pallas import tpu as pltpu
from jax.sharding import PartitionSpec as P

sigma_xy = 3.0
sigma_z = 1.5
reach = 8
tap_total = sum([math.exp(-((float(e) / sigma_xy) ** 2)) for e in range(-8, 9)])
MESH = pl.DeviceIdType.MESH
VM = pl.BlockSpec(memory_space=pltpu.VMEM)
ANY = pl.BlockSpec(memory_space=pl.ANY)
LIMIT = 48 * 1024 * 1024
WIDE = 58 * 1024 * 1024
f32 = jnp.float32
bf16 = jnp.bfloat16


def iota(shape, dim):
    return lax.broadcasted_iota(jnp.int32, shape, dim)


def dot_nt(a, b, precision=None):
    return lax.dot_general(a, b, (((1,), (1,)), ((), ())), precision=precision, preferred_element_type=f32)


def arc_tangent(n, t):
    small, large = jnp.minimum(n, t), jnp.maximum(n, t)
    upper = small > 0.41421356 * large
    r = jnp.where(upper, small - large, small) / jnp.where(upper, small + large, large)
    q = r * r
    poly = ((8.05374449538e-2 * q - 1.38776856032e-1) * q + 1.99777106478e-1) * q - 3.33329491539e-1
    angle = jnp.where(upper, math.pi / 4, 0.0) + (poly * q * r + r)
    return jnp.where(n > t, math.pi / 2 - angle, angle)


def flat(ref):
    return ref[...].reshape(1, ref.shape[0])


def pack_kernel(
    tiles, cap, half, inflow_ref, chord_ref, twist_ref, compliance_ref, frame_ref, owner_ref, cells_ref, out_ref, slot_ref, split_ref, packed_ref
):
    points = owner_ref.shape[1]
    step = 256
    tri = (iota((step, step), 0) < iota((step, step), 1)).astype(f32).astype(bf16)
    carry = jnp.zeros((tiles, 1), f32)
    mine = lax.axis_index("gz") * half
    wide = -(-cap // 128) * 128
    for k in range(points // step):
        here = owner_ref[:, k * step : (k + 1) * step]
        hot = (iota((tiles, step), 0) == here).astype(f32)
        rank = jnp.dot(hot.astype(bf16), tri, preferred_element_type=f32)
        position = jnp.sum(hot * (rank + carry), axis=0, keepdims=True)
        carry = carry + jnp.sum(hot, axis=1, keepdims=True)
        slot_ref[:, k * step : (k + 1) * step] = position.astype(jnp.int32) + (here - mine) * wide
    normal, tangent = inflow_ref[0:1, :], inflow_ref[1:2, :]
    speed_sq = normal * normal + tangent * tangent
    attack = arc_tangent(normal, tangent) - (flat(twist_ref) + flat(compliance_ref) * speed_sq)
    pressure = 0.5 * speed_sq * flat(chord_ref)
    lift = pressure * (2.0 * math.pi) * jnp.sin(attack)
    drag = pressure * (0.01 + 0.5 * attack * attack)
    channels = frame_ref.shape[0] // 2
    forces = frame_ref[:channels, :] * lift + frame_ref[channels:, :] * drag
    high = forces.astype(bf16).astype(f32)
    cells = jnp.concatenate([cells_ref[...].astype(f32), jnp.zeros((13, points), f32)], axis=0)
    split_ref[0:16, :] = jnp.concatenate([high, forces - high], axis=0).astype(bf16)
    split_ref[16:32, :] = cells.astype(bf16)
    block = 512
    slots = packed_ref.shape[1]

    def one(j, unused):
        first = pl.multiple_of(j * block, block)
        total = jnp.zeros((32, block), f32)
        part = 768
        for k in range(points // part):
            goal = slot_ref[:, k * part : (k + 1) * part] - first
            hot = jnp.where(iota((block, part), 0) == goal, 1.0, 0.0).astype(bf16)
            total = total + dot_nt(split_ref[:, k * part : (k + 1) * part], hot)
        packed_ref[0:8, pl.ds(first, block)] = total[0:8] + total[8:16]
        packed_ref[8:16, pl.ds(first, block)] = total[16:24]
        return unused

    lax.fori_loop(0, slots // block, one, 0)
    pieces = wide // 128
    for t in range(half):
        out_ref[t] = jnp.zeros(out_ref.shape[1:], f32)
        out_ref[t, :, 0:wide] = packed_ref[0:8, t * wide : (t + 1) * wide]
        for i in range(3):
            for j in range(pieces):
                row = i * pieces + j
                out_ref[t, row % 8 : row % 8 + 1, wide + row // 8 * 128 : wide + row // 8 * 128 + 128] = packed_ref[
                    8 + i : 9 + i, t * wide + j * 128 : t * wide + (j + 1) * 128
                ]


def points_kernel(tiles, cap, half, ny, in_ref, out_ref, land, send_sem, recv_sem, out_sem, pass_sem, own_sem):
    g, x, y, z = place()
    me = x * ny + y
    owns = me // half == z
    barrier = pltpu.get_barrier_semaphore()

    def device(t):
        return (g, t // ny, t % ny, z)

    sibling = (g, x, y, 1 - z)

    @pl.when(owns)
    def _():
        def greet(k, unused):
            pl.semaphore_signal(barrier, inc=1, device_id=device(lax.rem(me + k, tiles)), device_id_type=MESH)
            return unused

        lax.fori_loop(1, tiles, greet, 0)

    pl.semaphore_signal(barrier, inc=1, device_id=sibling, device_id_type=MESH)
    pl.semaphore_wait(barrier, half + 1 - owns.astype(jnp.int32))

    def send(k):
        far = z * half + lax.rem(me + k, half)
        return far, pltpu.make_async_remote_copy(
            src_ref=in_ref.at[far - z * half], dst_ref=land.at[me], send_sem=send_sem.at[k], recv_sem=recv_sem.at[me],
            device_id=device(far), device_id_type=MESH,
        )

    def hand(s):
        return pltpu.make_async_remote_copy(
            src_ref=land.at[s], dst_ref=land.at[s], send_sem=out_sem.at[s], recv_sem=pass_sem.at[s],
            device_id=sibling, device_id_type=MESH,
        )

    def start(k, unused):
        far, copy = send(k)

        @pl.when(far != me)
        def _():
            copy.start()

        return unused

    lax.fori_loop(0, half, start, 0)

    @pl.when(owns)
    def _():
        own = pltpu.make_async_copy(in_ref.at[me - z * half], land.at[me], own_sem)
        own.start()
        own.wait()
        hand(me).start()

        def take(k, unused):
            s = lax.rem(me + k, tiles)
            pltpu.make_async_remote_copy(
                src_ref=in_ref.at[0], dst_ref=land.at[s], send_sem=send_sem.at[0], recv_sem=recv_sem.at[s],
                device_id=device(s), device_id_type=MESH,
            ).wait_recv()
            hand(s).start()
            return unused

        lax.fori_loop(1, tiles, take, 0)

        def sent(s, unused):
            hand(s).wait_send()
            return unused

        lax.fori_loop(0, tiles, sent, 0)

    @pl.when(jnp.logical_not(owns))
    def _():
        def got(s, unused):
            hand(s).wait_recv()
            return unused

        lax.fori_loop(0, tiles, got, 0)

    def finish(k, unused):
        far, copy = send(k)

        @pl.when(far != me)
        def _():
            copy.wait_send()

        return unused

    lax.fori_loop(0, half, finish, 0)
    wide = -(-cap // 128) * 128
    pieces = wide // 128
    if out_ref.shape[1] > tiles * cap:
        out_ref[...] = jnp.zeros(out_ref.shape, f32)
    for s in range(tiles):
        out_ref[0:8, s * cap : (s + 1) * cap] = land[s, :, 0:cap]
        for i in range(3):
            for j in range(pieces):
                row = i * pieces + j
                size = min(128, cap - j * 128)
                out_ref[8 + i : 9 + i, s * cap + j * 128 : s * cap + j * 128 + size] = land[
                    s, row % 8 : row % 8 + 1, wide + row // 8 * 128 : wide + row // 8 * 128 + size
                ]


def tap_weight(offset):
    scaled = offset.astype(f32) * (1.0 / sigma_xy)
    return jnp.where(jnp.abs(offset) <= reach, jnp.exp(-scaled * scaled) * (1.0 / tap_total), 0.0)


def smear_kernel(
    sources, cap, channels, levels, levels_all, wx, wy, rows_ref, center_ref, xs_ref, ys_ref, cn_ref, a_ref, b_ref, h_ref, acc_ref, hacc_ref
):
    px = wx + 16
    first_level = lax.axis_index("gz") * levels
    acc_ref[...] = jnp.zeros(acc_ref.shape, f32)
    hacc_ref[...] = jnp.zeros(hacc_ref.shape, f32)
    folds, chunk = a_ref.shape[0], a_ref.shape[2]

    def fill(j, i):
        lanes = pl.ds(pl.multiple_of(j * chunk, chunk), chunk)
        cells = rows_ref[8:11, lanes].astype(jnp.int32)
        x, y, z = cells[0:1], cells[1:2], cells[2:3]
        gx = tap_weight(iota((px, chunk), 0) - reach - x)
        for c in range(channels):
            a_ref[i, c * px : (c + 1) * px, :] = (rows_ref[c : c + 1, lanes] * gx).astype(bf16)
        every = (iota((levels_all, chunk), 0) - z).astype(f32) * (1.0 / sigma_z)
        total = 1.0 / jnp.sum(jnp.exp(-every * every), axis=0, keepdims=True)
        gy = tap_weight(iota((wy + 16, chunk), 0) - reach - y).astype(bf16).astype(f32)
        for k in range(levels):
            near = (first_level + k - z).astype(f32) * (1.0 / sigma_z)
            gz = jnp.exp(-near * near) * total
            b_ref[i, k * wy : (k + 1) * wy, :] = (gy[8 : 8 + wy] * gz).astype(bf16)
            rims = jnp.concatenate([gy[0:8] * gz, gy[8 + wy :] * gz], axis=0)
            h_ref[i, k * 16 : (k + 1) * 16, :] = rims.astype(bf16)

    def add(i):
        acc_ref[...] += dot_nt(a_ref[i], b_ref[i])
        hacc_ref[...] += dot_nt(h_ref[i], a_ref[i])

    count = rows_ref.shape[1] // chunk
    fill(0, 0)

    def one(j, unused):
        for i in range(folds):
            fill(jnp.minimum(j * folds + i + 1, count - 1), (i + 1) % folds)
            add(i)
        return unused

    lax.fori_loop(0, count // folds, one, 0)
    for i in range(count % folds):
        if i + 1 < count % folds:
            fill(count - count % folds + i + 1, i + 1)
        add(i)
    for c in range(channels):
        center_ref[c] = acc_ref[c * px + 8 : c * px + 8 + wx, :]
        xs_ref[0, c] = acc_ref[c * px : c * px + 8, :]
        xs_ref[1, c] = acc_ref[c * px + 8 + wx : (c + 1) * px, :]
        for k in range(levels):
            for side in range(2):
                rim = hacc_ref[k * 16 + side * 8 : k * 16 + side * 8 + 8, c * px : (c + 1) * px]
                ys_ref[side, c, k * 8 : (k + 1) * 8, :] = rim[:, 8 : 8 + wx]
                cn_ref[side, 0, k * 8 : (k + 1) * 8, c * 8 : (c + 1) * 8] = rim[:, 0:8]
                cn_ref[side, 1, k * 8 : (k + 1) * 8, c * 8 : (c + 1) * 8] = rim[:, 8 + wx :]


def place():
    return (lax.axis_index("group"), lax.axis_index("gx"), lax.axis_index("gy"), lax.axis_index("gz"))


def rim_kernel(nx, ny, xs_ref, ys_ref, cn_ref, rx_ref, ry_ref, rc_ref, send_sem, recv_sem):
    g, x, y, z = place()
    barrier = pltpu.get_barrier_semaphore()
    moves = [(dx, dy) for dx in (-1, 0, 1) for dy in (-1, 0, 1) if (dx, dy) != (0, 0)]

    def there(dx, dy):
        return (x + dx >= 0) & (x + dx < nx) & (y + dy >= 0) & (y + dy < ny)

    def copy(i, dx, dy):
        high_x, high_y = (dx + 1) // 2, (dy + 1) // 2
        if dy == 0:
            src, dst = xs_ref.at[high_x], rx_ref.at[1 - high_x]
        elif dx == 0:
            src, dst = ys_ref.at[high_y], ry_ref.at[1 - high_y]
        else:
            src, dst = cn_ref.at[high_y, high_x], rc_ref.at[1 - high_y, 1 - high_x]
        return pltpu.make_async_remote_copy(
            src_ref=src, dst_ref=dst, send_sem=send_sem.at[i], recv_sem=recv_sem.at[i],
            device_id=(g, x + dx, y + dy, z), device_id_type=MESH,
        )

    count = jnp.int32(0)
    for dx, dy in moves:
        count = count + there(dx, dy).astype(jnp.int32)

        @pl.when(there(dx, dy))
        def _():
            pl.semaphore_signal(barrier, inc=1, device_id=(g, x + dx, y + dy, z), device_id_type=MESH)

    pl.semaphore_wait(barrier, count)
    for i, (dx, dy) in enumerate(moves):

        @pl.when(there(dx, dy))
        def _():
            copy(i, dx, dy).start()

    for i, (dx, dy) in enumerate(moves):

        @pl.when(there(dx, dy))
        def _():
            copy(i, dx, dy).wait_send()

        @pl.when(there(-dx, -dy))
        def _():
            copy(i, dx, dy).wait_recv()


def two(value, axis):
    high = value.astype(bf16)
    return jnp.concatenate([high, (value - high.astype(f32)).astype(bf16)], axis=axis)


def state_kernel(nx, ny, base_ref, tend_ref, center_ref, rx_ref, ry_ref, rc_ref, out_ref, uvw_ref, put_ref):
    unused_g, x, y, unused_z = place()
    c = pl.program_id(0)
    levels, wx, wy = base_ref.shape[1:]
    low_x, high_x, low_y, high_y = x > 0, x < nx - 1, y > 0, y < ny - 1
    strips = []
    for side, ok_y in ((0, low_y), (1, high_y)):
        strip = jnp.where(ok_y, ry_ref[side, 0], 0.0)
        for end, ok_x in ((0, low_x), (1, high_x)):
            corner = jnp.where(ok_y & ok_x, rc_ref[side, end], 0.0)
            size = corner.shape[1]
            row, col = iota((size, wx), 0), iota((size, wx), 1)
            put = ((row - c * 8 == col - end * (wx - 8)) & (row >= c * 8) & (row < c * 8 + 8)).astype(f32)
            strip = strip + jnp.dot(two(corner, 1), jnp.concatenate([put, put], axis=0).astype(bf16), preferred_element_type=f32)
        strips.append(strip)
    strip = jnp.concatenate(strips, axis=0)
    half = levels * 8

    @pl.when(c == 0)
    def _():
        row, col = iota((2 * half, levels * wy), 0), iota((2 * half, levels * wy), 1)
        side, level, cell = row // half, (row % half) // 8, row % 8
        put = (col == level * wy + cell + side * (wy - 8)).astype(f32)
        put_ref[...] = jnp.concatenate([put, put], axis=0).astype(bf16)

    source = center_ref[0] + lax.dot_general(two(strip, 0), put_ref[...], (((0,), (0,)), ((), ())), preferred_element_type=f32)
    source = jnp.concatenate(
        [
            source[:8] + jnp.where(low_x, rx_ref[0, 0], 0.0),
            source[8:-8],
            source[-8:] + jnp.where(high_x, rx_ref[1, 0], 0.0),
        ],
        axis=0,
    )
    for k in range(levels):
        value = base_ref[0, k] + 0.5 * (tend_ref[0, k].astype(f32) + source[:, k * wy : (k + 1) * wy])
        out_ref[0, k] = value

        @pl.when(c < 3)
        def _():
            uvw_ref[jnp.minimum(c, 2), k] = value


def lines_kernel(nx, ny, nz, fs_ref, out_ref, su, sv, ru, rv, rw, lines, land, hs, hr, ls, lr):
    g, x, y, z = place()
    unused, levels, wx, wy = fs_ref.shape
    barrier = pltpu.get_barrier_semaphore()

    def at(axis, d):
        return (g, x + d if axis == 0 else x, y + d if axis == 1 else y, z + d if axis == 2 else z)

    def there(axis, d):
        here, count = ((x, nx), (y, ny), (z, nz))[axis]
        return (here + d >= 0) & (here + d < count)

    for k in range(1, nx):
        pl.semaphore_signal(barrier, inc=1, device_id=(g, lax.rem(x + k, nx), y, z), device_id_type=MESH)
    count = jnp.int32(nx - 1)
    for axis in (1, 2):
        for d in (-1, 1):
            count = count + there(axis, d).astype(jnp.int32)

            @pl.when(there(axis, d))
            def _():
                pl.semaphore_signal(barrier, inc=1, device_id=at(axis, d), device_id_type=MESH)

    across = [jnp.transpose(fs_ref[1, k]) for k in range(levels)]
    for k in range(levels):
        su[0, k : k + 1, :] = fs_ref[0, k, 0:1, :]
        su[1, k : k + 1, :] = fs_ref[0, k, wx - 1 : wx, :]
        sv[0, k : k + 1, :] = across[k][0:1]
        sv[1, k : k + 1, :] = across[k][wy - 1 : wy]
    pl.semaphore_wait(barrier, count)

    def halo(axis, d):
        i = axis * 2 + (d + 1) // 2
        high = (d + 1) // 2
        if axis == 0:
            src, dst = su.at[high], ru.at[1 - high]
        elif axis == 1:
            src, dst = sv.at[high], rv.at[1 - high]
        else:
            src, dst = fs_ref.at[2, (levels - 1) * high], rw.at[1 - high]
        return pltpu.make_async_remote_copy(
            src_ref=src, dst_ref=dst, send_sem=hs.at[i], recv_sem=hr.at[i], device_id=at(axis, d), device_id_type=MESH
        )

    moves = [(axis, d) for axis in range(3) for d in (-1, 1)]
    for axis, d in moves:

        @pl.when(there(axis, d))
        def _():
            halo(axis, d).start()

        @pl.when(jnp.logical_not(there(axis, d)))
        def _():
            into = (ru, rv, rw)[axis]
            into[(d + 1) // 2] = jnp.zeros(into.shape[1:], f32)

    for axis, d in moves:

        @pl.when(there(axis, d))
        def _():
            halo(axis, d).wait_send()

        @pl.when(there(axis, -d))
        def _():
            halo(axis, d).wait_recv()

    band = wy // nx
    for k in range(levels):
        u = fs_ref[0, k]
        along = jnp.concatenate([u[1:], ru[1, k : k + 1, :]], axis=0) - jnp.concatenate([ru[0, k : k + 1, :], u[:-1]], axis=0)
        above = fs_ref[2, k + 1] if k + 1 < levels else rw[1]
        below = fs_ref[2, k - 1] if k > 0 else rw[0]
        v = across[k]
        over = jnp.concatenate([v[1:], rv[1, k : k + 1, :]], axis=0) - jnp.concatenate([rv[0, k : k + 1, :], v[:-1]], axis=0)
        div = 0.5 * (jnp.transpose(along + (above - below)) + over)
        for j in range(nx):
            lines[j, k] = div[j * band : (j + 1) * band]

    def line(k):
        far = lax.rem(x + k, nx)
        return pltpu.make_async_remote_copy(
            src_ref=lines.at[far], dst_ref=land.at[x], send_sem=ls.at[k], recv_sem=lr.at[k],
            device_id=(g, far, y, z), device_id_type=MESH,
        )

    def arrival(k):
        far = lax.rem(x + nx - k, nx)
        return pltpu.make_async_remote_copy(
            src_ref=lines.at[far], dst_ref=land.at[far], send_sem=ls.at[k], recv_sem=lr.at[k],
            device_id=(g, far, y, z), device_id_type=MESH,
        )

    for k in range(1, nx):
        line(k).start()
    land[x] = lines[x]
    for k in range(1, nx):
        line(k).wait_send()
        arrival(k).wait_recv()
    for j in range(nx):
        out_ref[:, :, j * wx : (j + 1) * wx] = land[j]


def params(collective_id=None, limit=LIMIT):
    if collective_id is None:
        return pltpu.CompilerParams(vmem_limit_bytes=limit)
    return pltpu.CompilerParams(vmem_limit_bytes=LIMIT, collective_id=collective_id, has_side_effects=True)


def body(base_state, tendency, inflow, chord_len, twist_base, compliance, blade_frame, owner_tile, point_cells):
    nx, ny, nz = lax.axis_size("gx"), lax.axis_size("gy"), lax.axis_size("gz")
    tiles = nx * ny
    points = owner_tile.shape[0]
    cap = max(2, (2 * points + tiles - 1) // tiles)
    channels, levels, wx, wy = base_state.shape
    px = wx + 16
    half = tiles // nz
    wide = -(-cap // 128) * 128
    slots = -(-tiles * cap // 512) * 512
    message = wide + -(-3 * (wide // 128) // 8) * 128
    shape = jax.ShapeDtypeStruct
    packed = pl.pallas_call(
        functools.partial(pack_kernel, tiles, cap, half),
        out_shape=shape((half, 8, message), f32),
        grid=(1,),
        in_specs=[
            pl.BlockSpec((2, points), lambda i: (0, 0)),
            pl.BlockSpec((points,), lambda i: (0,)),
            pl.BlockSpec((points,), lambda i: (0,)),
            pl.BlockSpec((points,), lambda i: (0,)),
            pl.BlockSpec(blade_frame.shape, lambda i: (0, 0)),
            pl.BlockSpec((1, points), lambda i: (0, 0)),
            pl.BlockSpec(point_cells.shape, lambda i: (0, 0)),
        ],
        out_specs=VM,
        scratch_shapes=[
            pltpu.VMEM((1, points), jnp.int32),
            pltpu.VMEM((32, points), bf16),
            pltpu.VMEM((16, -(-half * wide // 512) * 512), f32),
        ],
        compiler_params=params(limit=WIDE),
        name="pack_points",
    )(
        inflow,
        chord_len,
        twist_base,
        compliance,
        blade_frame,
        owner_tile.reshape(1, points),
        point_cells,
    )
    arrived = pl.pallas_call(
        functools.partial(points_kernel, tiles, cap, half, ny),
        out_shape=shape((16, slots), f32),
        in_specs=[ANY],
        out_specs=VM,
        scratch_shapes=[
            pltpu.VMEM((tiles, 8, message), f32),
            pltpu.SemaphoreType.DMA((half,)),
            pltpu.SemaphoreType.DMA((tiles,)),
            pltpu.SemaphoreType.DMA((tiles,)),
            pltpu.SemaphoreType.DMA((tiles,)),
            pltpu.SemaphoreType.DMA,
        ],
        compiler_params=params(0),
        name="exchange_points",
    )(packed)
    chunk = 512
    center, xs, ys, cn = pl.pallas_call(
        functools.partial(smear_kernel, tiles, cap, channels, levels, levels * nz, wx, wy),
        out_shape=(
            shape((channels, wx, levels * wy), f32),
            shape((2, channels, 8, levels * wy), f32),
            shape((2, channels, levels * 8, wx), f32),
            shape((2, 2, levels * 8, channels * 8), f32),
        ),
        in_specs=[VM],
        out_specs=(VM,) * 4,
        scratch_shapes=[
            pltpu.VMEM((2, channels * px, chunk), bf16),
            pltpu.VMEM((2, levels * wy, chunk), bf16),
            pltpu.VMEM((2, levels * 16, chunk), bf16),
            pltpu.VMEM((channels * px, levels * wy), f32),
            pltpu.VMEM((levels * 16, channels * px), f32),
        ],
        compiler_params=params(),
        name="smear_points",
    )(arrived)
    rx, ry, rc = pl.pallas_call(
        functools.partial(rim_kernel, nx, ny),
        out_shape=(shape(xs.shape, f32), shape(ys.shape, f32), shape(cn.shape, f32)),
        in_specs=[ANY] * 3,
        out_specs=(ANY,) * 3,
        scratch_shapes=[pltpu.SemaphoreType.DMA((8,)), pltpu.SemaphoreType.DMA((8,))],
        compiler_params=params(1),
        name="exchange_rims",
    )(xs, ys, cn)
    forced_state, velocity = pl.pallas_call(
        functools.partial(state_kernel, nx, ny),
        grid=(channels,),
        out_shape=(shape(base_state.shape, f32), shape((3, levels, wx, wy), f32)),
        in_specs=[
            pl.BlockSpec((1, levels, wx, wy), lambda c: (c, 0, 0, 0)),
            pl.BlockSpec((1, levels, wx, wy), lambda c: (c, 0, 0, 0)),
            pl.BlockSpec((1, wx, levels * wy), lambda c: (c, 0, 0)),
            pl.BlockSpec((2, 1, 8, levels * wy), lambda c: (0, c, 0, 0)),
            pl.BlockSpec((2, 1, levels * 8, wx), lambda c: (0, c, 0, 0)),
            pl.BlockSpec(cn.shape, lambda c: (0, 0, 0, 0)),
        ],
        out_specs=(pl.BlockSpec((1, levels, wx, wy), lambda c: (c, 0, 0, 0)), VM),
        scratch_shapes=[pltpu.VMEM((4 * levels * 8, levels * wy), bf16)],
        compiler_params=params(),
        name="forced_state",
    )(base_state, tendency, center, rx, ry, rc)
    band = wy // nx
    divergence_lines = pl.pallas_call(
        functools.partial(lines_kernel, nx, ny, nz),
        out_shape=shape((levels, band, nx * wx), f32),
        in_specs=[VM],
        out_specs=VM,
        scratch_shapes=[
            pltpu.VMEM((2, levels, wy), f32),
            pltpu.VMEM((2, levels, wx), f32),
            pltpu.VMEM((2, levels, wy), f32),
            pltpu.VMEM((2, levels, wx), f32),
            pltpu.VMEM((2, wx, wy), f32),
            pltpu.VMEM((nx, levels, band, wx), f32),
            pltpu.VMEM((nx, levels, band, wx), f32),
            pltpu.SemaphoreType.DMA((6,)),
            pltpu.SemaphoreType.DMA((6,)),
            pltpu.SemaphoreType.DMA((nx,)),
            pltpu.SemaphoreType.DMA((nx,)),
        ],
        compiler_params=params(2),
        name="divergence_lines",
    )(velocity)
    return (forced_state, divergence_lines)


def solution(mesh):
    in_specs = (
        P("group", "gz", "gx", "gy"),
        P("group", "gz", "gx", "gy"),
        P("group", ("gx", "gy")),
        P(("group", "gx", "gy")),
        P(("group", "gx", "gy")),
        P(("group", "gx", "gy")),
        P("group", ("gx", "gy")),
        P(("gx", "gy"), "group"),
        P("group", ("gx", "gy")),
    )
    out_specs = (P("group", "gz", "gx", "gy"), P(("group", "gz"), ("gy", "gx"), None))
    return jax.shard_map(body, mesh=mesh, in_specs=in_specs, out_specs=out_specs, check_vma=False)
```

```python
import functools
import math

import jax
import jax.numpy as jnp
from jax import lax
from jax.experimental import pallas as pl
from jax.experimental.pallas import tpu as pltpu
from jax.sharding import PartitionSpec as P

sigma_xy = 3.0
sigma_z = 1.5
reach = 8
tap_total = sum([math.exp(-((float(e) / sigma_xy) ** 2)) for e in range(-8, 9)])
MESH = pl.DeviceIdType.MESH
VM = pl.BlockSpec(memory_space=pltpu.VMEM)
ANY = pl.BlockSpec(memory_space=pl.ANY)
LIMIT = 48 * 1024 * 1024
WIDE = 58 * 1024 * 1024
f32 = jnp.float32
bf16 = jnp.bfloat16


def iota(shape, dim):
    return lax.broadcasted_iota(jnp.int32, shape, dim)


def dot_nt(a, b, precision=None):
    return lax.dot_general(a, b, (((1,), (1,)), ((), ())), precision=precision, preferred_element_type=f32)


def arc_tangent(n, t):
    small, large = jnp.minimum(n, t), jnp.maximum(n, t)
    upper = small > 0.41421356 * large
    r = jnp.where(upper, small - large, small) / jnp.where(upper, small + large, large)
    q = r * r
    poly = ((8.05374449538e-2 * q - 1.38776856032e-1) * q + 1.99777106478e-1) * q - 3.33329491539e-1
    angle = jnp.where(upper, math.pi / 4, 0.0) + (poly * q * r + r)
    return jnp.where(n > t, math.pi / 2 - angle, angle)


def flat(ref):
    return ref[...].reshape(1, ref.shape[0])


def pack_kernel(
    tiles, cap, half, inflow_ref, chord_ref, twist_ref, compliance_ref, frame_ref, owner_ref, cells_ref, out_ref, slot_ref, split_ref, packed_ref
):
    points = owner_ref.shape[1]
    step = 256
    tri = (iota((step, step), 0) < iota((step, step), 1)).astype(f32).astype(bf16)
    carry = jnp.zeros((tiles, 1), f32)
    mine = lax.axis_index("gz") * half
    wide = -(-cap // 128) * 128
    for k in range(points // step):
        here = owner_ref[:, k * step : (k + 1) * step]
        hot = (iota((tiles, step), 0) == here).astype(f32)
        rank = jnp.dot(hot.astype(bf16), tri, preferred_element_type=f32)
        position = jnp.sum(hot * (rank + carry), axis=0, keepdims=True)
        carry = carry + jnp.sum(hot, axis=1, keepdims=True)
        slot_ref[:, k * step : (k + 1) * step] = position.astype(jnp.int32) + (here - mine) * wide
    normal, tangent = inflow_ref[0:1, :], inflow_ref[1:2, :]
    speed_sq = normal * normal + tangent * tangent
    attack = arc_tangent(normal, tangent) - (flat(twist_ref) + flat(compliance_ref) * speed_sq)
    pressure = 0.5 * speed_sq * flat(chord_ref)
    lift = pressure * (2.0 * math.pi) * jnp.sin(attack)
    drag = pressure * (0.01 + 0.5 * attack * attack)
    channels = frame_ref.shape[0] // 2
    forces = frame_ref[:channels, :] * lift + frame_ref[channels:, :] * drag
    high = forces.astype(bf16).astype(f32)
    cells = jnp.concatenate([cells_ref[...].astype(f32), jnp.zeros((13, points), f32)], axis=0)
    split_ref[0:16, :] = jnp.concatenate([high, forces - high], axis=0).astype(bf16)
    split_ref[16:32, :] = cells.astype(bf16)
    block = 512
    slots = packed_ref.shape[1]

    def one(j, unused):
        first = pl.multiple_of(j * block, block)
        total = jnp.zeros((32, block), f32)
        part = 768
        for k in range(points // part):
            goal = slot_ref[:, k * part : (k + 1) * part] - first
            hot = jnp.where(iota((block, part), 0) == goal, 1.0, 0.0).astype(bf16)
            total = total + dot_nt(split_ref[:, k * part : (k + 1) * part], hot)
        packed_ref[0:8, pl.ds(first, block)] = total[0:8] + total[8:16]
        packed_ref[8:16, pl.ds(first, block)] = total[16:24]
        return unused

    lax.fori_loop(0, slots // block, one, 0)
    pieces = wide // 128
    for t in range(half):
        out_ref[t] = jnp.zeros(out_ref.shape[1:], f32)
        out_ref[t, :, 0:wide] = packed_ref[0:8, t * wide : (t + 1) * wide]
        for i in range(3):
            for j in range(pieces):
                row = i * pieces + j
                out_ref[t, row % 8 : row % 8 + 1, wide + row // 8 * 128 : wide + row // 8 * 128 + 128] = packed_ref[
                    8 + i : 9 + i, t * wide + j * 128 : t * wide + (j + 1) * 128
                ]


def points_kernel(tiles, cap, half, ny, in_ref, out_ref, land, send_sem, recv_sem, out_sem, pass_sem, own_sem):
    g, x, y, z = place()
    me = x * ny + y
    owns = me // half == z
    barrier = pltpu.get_barrier_semaphore()

    def device(t):
        return (g, t // ny, t % ny, z)

    sibling = (g, x, y, 1 - z)

    @pl.when(owns)
    def _():
        def greet(k, unused):
            pl.semaphore_signal(barrier, inc=1, device_id=device(lax.rem(me + k, tiles)), device_id_type=MESH)
            return unused

        lax.fori_loop(1, tiles, greet, 0)

    pl.semaphore_signal(barrier, inc=1, device_id=sibling, device_id_type=MESH)
    pl.semaphore_wait(barrier, half + 1 - owns.astype(jnp.int32))

    def send(k):
        far = z * half + lax.rem(me + k, half)
        return far, pltpu.make_async_remote_copy(
            src_ref=in_ref.at[far - z * half], dst_ref=land.at[me], send_sem=send_sem.at[k], recv_sem=recv_sem.at[me],
            device_id=device(far), device_id_type=MESH,
        )

    def hand(s):
        return pltpu.make_async_remote_copy(
            src_ref=land.at[s], dst_ref=land.at[s], send_sem=out_sem.at[s], recv_sem=pass_sem.at[s],
            device_id=sibling, device_id_type=MESH,
        )

    def start(k, unused):
        far, copy = send(k)

        @pl.when(far != me)
        def _():
            copy.start()

        return unused

    lax.fori_loop(0, half, start, 0)

    @pl.when(owns)
    def _():
        own = pltpu.make_async_copy(in_ref.at[me - z * half], land.at[me], own_sem)
        own.start()
        own.wait()
        hand(me).start()

        def take(k, unused):
            s = lax.rem(me + k, tiles)
            pltpu.make_async_remote_copy(
                src_ref=in_ref.at[0], dst_ref=land.at[s], send_sem=send_sem.at[0], recv_sem=recv_sem.at[s],
                device_id=device(s), device_id_type=MESH,
            ).wait_recv()
            hand(s).start()
            return unused

        lax.fori_loop(1, tiles, take, 0)

        def sent(s, unused):
            hand(s).wait_send()
            return unused

        lax.fori_loop(0, tiles, sent, 0)

    @pl.when(jnp.logical_not(owns))
    def _():
        def got(s, unused):
            hand(s).wait_recv()
            return unused

        lax.fori_loop(0, tiles, got, 0)

    def finish(k, unused):
        far, copy = send(k)

        @pl.when(far != me)
        def _():
            copy.wait_send()

        return unused

    lax.fori_loop(0, half, finish, 0)
    wide = -(-cap // 128) * 128
    pieces = wide // 128
    if out_ref.shape[1] > tiles * cap:
        out_ref[...] = jnp.zeros(out_ref.shape, f32)
    for s in range(tiles):
        out_ref[0:8, s * cap : (s + 1) * cap] = land[s, :, 0:cap]
        for i in range(3):
            for j in range(pieces):
                row = i * pieces + j
                size = min(128, cap - j * 128)
                out_ref[8 + i : 9 + i, s * cap + j * 128 : s * cap + j * 128 + size] = land[
                    s, row % 8 : row % 8 + 1, wide + row // 8 * 128 : wide + row // 8 * 128 + size
                ]


def tap_weight(offset):
    scaled = offset.astype(f32) * (1.0 / sigma_xy)
    return jnp.where(jnp.abs(offset) <= reach, jnp.exp(-scaled * scaled) * (1.0 / tap_total), 0.0)


def smear_kernel(
    sources, cap, channels, levels, levels_all, wx, wy, rows_ref, center_ref, xs_ref, ys_ref, cn_ref, a_ref, b_ref, h_ref, acc_ref, hacc_ref
):
    px = wx + 16
    first_level = lax.axis_index("gz") * levels
    acc_ref[...] = jnp.zeros(acc_ref.shape, f32)
    hacc_ref[...] = jnp.zeros(hacc_ref.shape, f32)
    folds, chunk = a_ref.shape[0], a_ref.shape[2]

    def fill(j, i):
        lanes = pl.ds(pl.multiple_of(j * chunk, chunk), chunk)
        cells = rows_ref[8:11, lanes].astype(jnp.int32)
        x, y, z = cells[0:1], cells[1:2], cells[2:3]
        gx = tap_weight(iota((px, chunk), 0) - reach - x)
        for c in range(channels):
            a_ref[i, c * px : (c + 1) * px, :] = (rows_ref[c : c + 1, lanes] * gx).astype(bf16)
        every = (iota((levels_all, chunk), 0) - z).astype(f32) * (1.0 / sigma_z)
        total = 1.0 / jnp.sum(jnp.exp(-every * every), axis=0, keepdims=True)
        gy = tap_weight(iota((wy + 16, chunk), 0) - reach - y).astype(bf16).astype(f32)
        for k in range(levels):
            near = (first_level + k - z).astype(f32) * (1.0 / sigma_z)
            gz = jnp.exp(-near * near) * total
            b_ref[i, k * wy : (k + 1) * wy, :] = (gy[8 : 8 + wy] * gz).astype(bf16)
            rims = jnp.concatenate([gy[0:8] * gz, gy[8 + wy :] * gz], axis=0)
            h_ref[i, k * 16 : (k + 1) * 16, :] = rims.astype(bf16)

    def add(i):
        acc_ref[...] += dot_nt(a_ref[i], b_ref[i])
        hacc_ref[...] += dot_nt(h_ref[i], a_ref[i])

    count = rows_ref.shape[1] // chunk
    fill(0, 0)

    def one(j, unused):
        for i in range(folds):
            fill(jnp.minimum(j * folds + i + 1, count - 1), (i + 1) % folds)
            add(i)
        return unused

    lax.fori_loop(0, count // folds, one, 0)
    for i in range(count % folds):
        if i + 1 < count % folds:
            fill(count - count % folds + i + 1, i + 1)
        add(i)
    for c in range(channels):
        center_ref[c] = acc_ref[c * px + 8 : c * px + 8 + wx, :]
        xs_ref[0, c] = acc_ref[c * px : c * px + 8, :]
        xs_ref[1, c] = acc_ref[c * px + 8 + wx : (c + 1) * px, :]
        for k in range(levels):
            for side in range(2):
                rim = hacc_ref[k * 16 + side * 8 : k * 16 + side * 8 + 8, c * px : (c + 1) * px]
                ys_ref[side, c, k * 8 : (k + 1) * 8, :] = rim[:, 8 : 8 + wx]
                cn_ref[side, 0, k * 8 : (k + 1) * 8, c * 8 : (c + 1) * 8] = rim[:, 0:8]
                cn_ref[side, 1, k * 8 : (k + 1) * 8, c * 8 : (c + 1) * 8] = rim[:, 8 + wx :]


def place():
    return (lax.axis_index("group"), lax.axis_index("gx"), lax.axis_index("gy"), lax.axis_index("gz"))


def rim_kernel(nx, ny, xs_ref, ys_ref, cn_ref, rx_ref, ry_ref, rc_ref, send_sem, recv_sem):
    g, x, y, z = place()
    barrier = pltpu.get_barrier_semaphore()
    moves = [(dx, dy) for dx in (-1, 0, 1) for dy in (-1, 0, 1) if (dx, dy) != (0, 0)]

    def there(dx, dy):
        return (x + dx >= 0) & (x + dx < nx) & (y + dy >= 0) & (y + dy < ny)

    def copy(i, dx, dy):
        high_x, high_y = (dx + 1) // 2, (dy + 1) // 2
        if dy == 0:
            src, dst = xs_ref.at[high_x], rx_ref.at[1 - high_x]
        elif dx == 0:
            src, dst = ys_ref.at[high_y], ry_ref.at[1 - high_y]
        else:
            src, dst = cn_ref.at[high_y, high_x], rc_ref.at[1 - high_y, 1 - high_x]
        return pltpu.make_async_remote_copy(
            src_ref=src, dst_ref=dst, send_sem=send_sem.at[i], recv_sem=recv_sem.at[i],
            device_id=(g, x + dx, y + dy, z), device_id_type=MESH,
        )

    count = jnp.int32(0)
    for dx, dy in moves:
        count = count + there(dx, dy).astype(jnp.int32)

        @pl.when(there(dx, dy))
        def _():
            pl.semaphore_signal(barrier, inc=1, device_id=(g, x + dx, y + dy, z), device_id_type=MESH)

    pl.semaphore_wait(barrier, count)
    for i, (dx, dy) in enumerate(moves):

        @pl.when(there(dx, dy))
        def _():
            copy(i, dx, dy).start()

    for i, (dx, dy) in enumerate(moves):

        @pl.when(there(dx, dy))
        def _():
            copy(i, dx, dy).wait_send()

        @pl.when(there(-dx, -dy))
        def _():
            copy(i, dx, dy).wait_recv()


def two(value, axis):
    high = value.astype(bf16)
    return jnp.concatenate([high, (value - high.astype(f32)).astype(bf16)], axis=axis)


def state_kernel(nx, ny, base_ref, tend_ref, center_ref, rx_ref, ry_ref, rc_ref, out_ref, uvw_ref, put_ref):
    unused_g, x, y, unused_z = place()
    c = pl.program_id(0)
    levels, wx, wy = base_ref.shape[1:]
    low_x, high_x, low_y, high_y = x > 0, x < nx - 1, y > 0, y < ny - 1
    strips = []
    for side, ok_y in ((0, low_y), (1, high_y)):
        strip = jnp.where(ok_y, ry_ref[side, 0], 0.0)
        for end, ok_x in ((0, low_x), (1, high_x)):
            corner = jnp.where(ok_y & ok_x, rc_ref[side, end], 0.0)
            size = corner.shape[1]
            row, col = iota((size, wx), 0), iota((size, wx), 1)
            put = ((row - c * 8 == col - end * (wx - 8)) & (row >= c * 8) & (row < c * 8 + 8)).astype(f32)
            strip = strip + jnp.dot(two(corner, 1), jnp.concatenate([put, put], axis=0).astype(bf16), preferred_element_type=f32)
        strips.append(strip)
    strip = jnp.concatenate(strips, axis=0)
    half = levels * 8

    @pl.when(c == 0)
    def _():
        row, col = iota((2 * half, levels * wy), 0), iota((2 * half, levels * wy), 1)
        side, level, cell = row // half, (row % half) // 8, row % 8
        put = (col == level * wy + cell + side * (wy - 8)).astype(f32)
        put_ref[...] = jnp.concatenate([put, put], axis=0).astype(bf16)

    source = center_ref[0] + lax.dot_general(two(strip, 0), put_ref[...], (((0,), (0,)), ((), ())), preferred_element_type=f32)
    source = jnp.concatenate(
        [
            source[:8] + jnp.where(low_x, rx_ref[0, 0], 0.0),
            source[8:-8],
            source[-8:] + jnp.where(high_x, rx_ref[1, 0], 0.0),
        ],
        axis=0,
    )
    for k in range(levels):
        value = base_ref[0, k] + 0.5 * (tend_ref[0, k].astype(f32) + source[:, k * wy : (k + 1) * wy])
        out_ref[0, k] = value

        @pl.when(c < 3)
        def _():
            uvw_ref[jnp.minimum(c, 2), k] = value


def lines_kernel(nx, ny, nz, fs_ref, out_ref, su, sv, ru, rv, rw, lines, land, hs, hr, ls, lr):
    g, x, y, z = place()
    unused, levels, wx, wy = fs_ref.shape
    barrier = pltpu.get_barrier_semaphore()

    def at(axis, d):
        return (g, x + d if axis == 0 else x, y + d if axis == 1 else y, z + d if axis == 2 else z)

    def there(axis, d):
        here, count = ((x, nx), (y, ny), (z, nz))[axis]
        return (here + d >= 0) & (here + d < count)

    for k in range(1, nx):
        pl.semaphore_signal(barrier, inc=1, device_id=(g, lax.rem(x + k, nx), y, z), device_id_type=MESH)
    count = jnp.int32(nx - 1)
    for axis in (1, 2):
        for d in (-1, 1):
            count = count + there(axis, d).astype(jnp.int32)

            @pl.when(there(axis, d))
            def _():
                pl.semaphore_signal(barrier, inc=1, device_id=at(axis, d), device_id_type=MESH)

    across = [jnp.transpose(fs_ref[1, k]) for k in range(levels)]
    for k in range(levels):
        su[0, k : k + 1, :] = fs_ref[0, k, 0:1, :]
        su[1, k : k + 1, :] = fs_ref[0, k, wx - 1 : wx, :]
        sv[0, k : k + 1, :] = across[k][0:1]
        sv[1, k : k + 1, :] = across[k][wy - 1 : wy]
    pl.semaphore_wait(barrier, count)

    def halo(axis, d):
        i = axis * 2 + (d + 1) // 2
        high = (d + 1) // 2
        if axis == 0:
            src, dst = su.at[high], ru.at[1 - high]
        elif axis == 1:
            src, dst = sv.at[high], rv.at[1 - high]
        else:
            src, dst = fs_ref.at[2, (levels - 1) * high], rw.at[1 - high]
        return pltpu.make_async_remote_copy(
            src_ref=src, dst_ref=dst, send_sem=hs.at[i], recv_sem=hr.at[i], device_id=at(axis, d), device_id_type=MESH
        )

    moves = [(axis, d) for axis in range(3) for d in (-1, 1)]
    for axis, d in moves:

        @pl.when(there(axis, d))
        def _():
            halo(axis, d).start()

        @pl.when(jnp.logical_not(there(axis, d)))
        def _():
            into = (ru, rv, rw)[axis]
            into[(d + 1) // 2] = jnp.zeros(into.shape[1:], f32)

    for axis, d in moves:

        @pl.when(there(axis, d))
        def _():
            halo(axis, d).wait_send()

        @pl.when(there(axis, -d))
        def _():
            halo(axis, d).wait_recv()

    band = wy // nx
    for k in range(levels):
        u = fs_ref[0, k]
        along = jnp.concatenate([u[1:], ru[1, k : k + 1, :]], axis=0) - jnp.concatenate([ru[0, k : k + 1, :], u[:-1]], axis=0)
        above = fs_ref[2, k + 1] if k + 1 < levels else rw[1]
        below = fs_ref[2, k - 1] if k > 0 else rw[0]
        v = across[k]
        over = jnp.concatenate([v[1:], rv[1, k : k + 1, :]], axis=0) - jnp.concatenate([rv[0, k : k + 1, :], v[:-1]], axis=0)
        div = 0.5 * (jnp.transpose(along + (above - below)) + over)
        for j in range(nx):
            lines[j, k] = div[j * band : (j + 1) * band]

    def line(k):
        far = lax.rem(x + k, nx)
        return pltpu.make_async_remote_copy(
            src_ref=lines.at[far], dst_ref=land.at[x], send_sem=ls.at[k], recv_sem=lr.at[k],
            device_id=(g, far, y, z), device_id_type=MESH,
        )

    def arrival(k):
        far = lax.rem(x + nx - k, nx)
        return pltpu.make_async_remote_copy(
            src_ref=lines.at[far], dst_ref=land.at[far], send_sem=ls.at[k], recv_sem=lr.at[k],
            device_id=(g, far, y, z), device_id_type=MESH,
        )

    for k in range(1, nx):
        line(k).start()
    land[x] = lines[x]
    for k in range(1, nx):
        line(k).wait_send()
        arrival(k).wait_recv()
    for j in range(nx):
        out_ref[:, :, j * wx : (j + 1) * wx] = land[j]


def params(collective_id=None, limit=LIMIT):
    if collective_id is None:
        return pltpu.CompilerParams(vmem_limit_bytes=limit)
    return pltpu.CompilerParams(vmem_limit_bytes=LIMIT, collective_id=collective_id, has_side_effects=True)


def body(base_state, tendency, inflow, chord_len, twist_base, compliance, blade_frame, owner_tile, point_cells):
    nx, ny, nz = lax.axis_size("gx"), lax.axis_size("gy"), lax.axis_size("gz")
    tiles = nx * ny
    points = owner_tile.shape[0]
    cap = max(2, (2 * points + tiles - 1) // tiles)
    channels, levels, wx, wy = base_state.shape
    px = wx + 16
    half = tiles // nz
    wide = -(-cap // 128) * 128
    slots = -(-tiles * cap // 768) * 768
    message = wide + -(-3 * (wide // 128) // 8) * 128
    shape = jax.ShapeDtypeStruct
    packed = pl.pallas_call(
        functools.partial(pack_kernel, tiles, cap, half),
        out_shape=shape((half, 8, message), f32),
        grid=(1,),
        in_specs=[
            pl.BlockSpec((2, points), lambda i: (0, 0)),
            pl.BlockSpec((points,), lambda i: (0,)),
            pl.BlockSpec((points,), lambda i: (0,)),
            pl.BlockSpec((points,), lambda i: (0,)),
            pl.BlockSpec(blade_frame.shape, lambda i: (0, 0)),
            pl.BlockSpec((1, points), lambda i: (0, 0)),
            pl.BlockSpec(point_cells.shape, lambda i: (0, 0)),
        ],
        out_specs=VM,
        scratch_shapes=[
            pltpu.VMEM((1, points), jnp.int32),
            pltpu.VMEM((32, points), bf16),
            pltpu.VMEM((16, -(-half * wide // 512) * 512), f32),
        ],
        compiler_params=params(limit=WIDE),
        name="pack_points",
    )(
        inflow,
        chord_len,
        twist_base,
        compliance,
        blade_frame,
        owner_tile.reshape(1, points),
        point_cells,
    )
    arrived = pl.pallas_call(
        functools.partial(points_kernel, tiles, cap, half, ny),
        out_shape=shape((16, slots), f32),
        in_specs=[ANY],
        out_specs=VM,
        scratch_shapes=[
            pltpu.VMEM((tiles, 8, message), f32),
            pltpu.SemaphoreType.DMA((half,)),
            pltpu.SemaphoreType.DMA((tiles,)),
            pltpu.SemaphoreType.DMA((tiles,)),
            pltpu.SemaphoreType.DMA((tiles,)),
            pltpu.SemaphoreType.DMA,
        ],
        compiler_params=params(0),
        name="exchange_points",
    )(packed)
    chunk = 768
    center, xs, ys, cn = pl.pallas_call(
        functools.partial(smear_kernel, tiles, cap, channels, levels, levels * nz, wx, wy),
        out_shape=(
            shape((channels, wx, levels * wy), f32),
            shape((2, channels, 8, levels * wy), f32),
            shape((2, channels, levels * 8, wx), f32),
            shape((2, 2, levels * 8, channels * 8), f32),
        ),
        in_specs=[VM],
        out_specs=(VM,) * 4,
        scratch_shapes=[
            pltpu.VMEM((2, channels * px, chunk), bf16),
            pltpu.VMEM((2, levels * wy, chunk), bf16),
            pltpu.VMEM((2, levels * 16, chunk), bf16),
            pltpu.VMEM((channels * px, levels * wy), f32),
            pltpu.VMEM((levels * 16, channels * px), f32),
        ],
        compiler_params=params(),
        name="smear_points",
    )(arrived)
    rx, ry, rc = pl.pallas_call(
        functools.partial(rim_kernel, nx, ny),
        out_shape=(shape(xs.shape, f32), shape(ys.shape, f32), shape(cn.shape, f32)),
        in_specs=[ANY] * 3,
        out_specs=(ANY,) * 3,
        scratch_shapes=[pltpu.SemaphoreType.DMA((8,)), pltpu.SemaphoreType.DMA((8,))],
        compiler_params=params(1),
        name="exchange_rims",
    )(xs, ys, cn)
    forced_state, velocity = pl.pallas_call(
        functools.partial(state_kernel, nx, ny),
        grid=(channels,),
        out_shape=(shape(base_state.shape, f32), shape((3, levels, wx, wy), f32)),
        in_specs=[
            pl.BlockSpec((1, levels, wx, wy), lambda c: (c, 0, 0, 0)),
            pl.BlockSpec((1, levels, wx, wy), lambda c: (c, 0, 0, 0)),
            pl.BlockSpec((1, wx, levels * wy), lambda c: (c, 0, 0)),
            pl.BlockSpec((2, 1, 8, levels * wy), lambda c: (0, c, 0, 0)),
            pl.BlockSpec((2, 1, levels * 8, wx), lambda c: (0, c, 0, 0)),
            pl.BlockSpec(cn.shape, lambda c: (0, 0, 0, 0)),
        ],
        out_specs=(pl.BlockSpec((1, levels, wx, wy), lambda c: (c, 0, 0, 0)), VM),
        scratch_shapes=[pltpu.VMEM((4 * levels * 8, levels * wy), bf16)],
        compiler_params=params(),
        name="forced_state",
    )(base_state, tendency, center, rx, ry, rc)
    band = wy // nx
    divergence_lines = pl.pallas_call(
        functools.partial(lines_kernel, nx, ny, nz),
        out_shape=shape((levels, band, nx * wx), f32),
        in_specs=[VM],
        out_specs=VM,
        scratch_shapes=[
            pltpu.VMEM((2, levels, wy), f32),
            pltpu.VMEM((2, levels, wx), f32),
            pltpu.VMEM((2, levels, wy), f32),
            pltpu.VMEM((2, levels, wx), f32),
            pltpu.VMEM((2, wx, wy), f32),
            pltpu.VMEM((nx, levels, band, wx), f32),
            pltpu.VMEM((nx, levels, band, wx), f32),
            pltpu.SemaphoreType.DMA((6,)),
            pltpu.SemaphoreType.DMA((6,)),
            pltpu.SemaphoreType.DMA((nx,)),
            pltpu.SemaphoreType.DMA((nx,)),
        ],
        compiler_params=params(2),
        name="divergence_lines",
    )(velocity)
    return (forced_state, divergence_lines)


def solution(mesh):
    in_specs = (
        P("group", "gz", "gx", "gy"),
        P("group", "gz", "gx", "gy"),
        P("group", ("gx", "gy")),
        P(("group", "gx", "gy")),
        P(("group", "gx", "gy")),
        P(("group", "gx", "gy")),
        P("group", ("gx", "gy")),
        P(("gx", "gy"), "group"),
        P("group", ("gx", "gy")),
    )
    out_specs = (P("group", "gz", "gx", "gy"), P(("group", "gz"), ("gy", "gx"), None))
    return jax.shard_map(body, mesh=mesh, in_specs=in_specs, out_specs=out_specs, check_vma=False)
```
